512 devices in a mesh: dp: 32 (over x_hi, z), segment: 16 (over y, x_lo, core).
Axes of the slice: x: 4 (x_hi: 2, x_lo: 2; x = x_hi * 2 + x_lo), y: 4, z: 16, core: 2. Of those that a mesh axis runs over, the one named last changes fastest.
Arguments:
- features: bfloat16 [6144, 640], P('dp'), may hold values from -6 to 6
- timesteps: int32 [96], P('dp'), may hold values from 0 to 999
- text_ids: int32 [96, 64], replicated, may hold values from 0 to 16383
- text_table: bfloat16 [16384, 640], P(('dp', 'segment')), may hold values from -12 to 12
- in_weights: bfloat16 [16, 640, 640], P('segment'), may hold values from -0.25 to 0.25
- out_weights: bfloat16 [16, 640, 640], P('segment'), may hold values from -0.25 to 0.25
- skip_weights: bfloat16 [16, 640, 640], P('segment'), may hold values from -0.25 to 0.25
- cotangent: bfloat16 [6144, 640], P('dp'), may hold values from -0.076171875 to 0.076171875
Outputs:
- in_grads: float32 [16, 640, 640], P('segment', 'dp')
- out_grads: float32 [16, 640, 640], P('segment', 'dp')
- skip_grads: float32 [16, 640, 640], P('segment', 'dp')
The draws below stay inside these ranges and needn't reach their ends.
All inputs are finite; a program needn't handle non-finite values.
Results may differ from the reference program's by a relative error of at most 0.033.
Values may be sent and summed in bfloat16 or wider, within the bound.
A program may use at most 64 MiB of HBM per device.

```python
import math
import jax
import jax.numpy as jnp
import numpy as np
from jax import lax

C = 640
GROUPS = 32
MB = 3
TEXT_LEN = 64
VOCAB = 16384
ROWS = 64
BATCH = 96
N_DP = 32
N_SEGMENT = 16


def touch_ends(array, own_key, least, high):
    longest = array.shape.index(max(array.shape))
    spots = []
    for shift in (0, 1):
        where = [jax.random.randint(jax.random.fold_in(own_key, axis), (), 0, length) for axis, length in enumerate(array.shape)]
        where[longest] = (where[longest] + shift) % array.shape[longest]
        spots.append(tuple(where))
    return array.at[spots[0]].set(least).at[spots[1]].set(high)


def levels(rng, dims, cuts, low, largest):
    gain, own = 1.0, jax.random.fold_in(rng, 6)
    for dim, shards_of in cuts:
        draws = jnp.exp(jax.random.uniform(jax.random.fold_in(own, dim), (shards_of,), jnp.float32, low / len(cuts), largest / len(cuts)))
        gain = gain * jnp.repeat(draws, dims[dim] // shards_of).reshape([-1 if axis == dim else 1 for axis in range(len(dims))])
    return gain


def rank_bounds(number_of, lean):
    portions = [(1 << 20) // math.isqrt(standing ** lean) + 1 for standing in range(1, number_of + 1)]
    scale = 1 + sum(portions) // (1 << 30)
    return np.cumsum(np.array([max(1, weight // scale) for weight in portions]))


def ranked(key, dims, count, slope):
    listing = rank_bounds(count, slope)
    pick = jax.random.randint(jax.random.fold_in(key, 1), dims, 0, int(listing[count - 1]))
    rank = jnp.searchsorted(jnp.asarray(listing, jnp.int32), pick, side="right")
    return jax.random.permutation(jax.random.fold_in(key, 2), count)[rank].astype(jnp.int32)


def noise(rng, extent, deviation, limit, shards=(), held_as=jnp.bfloat16):
    entries = jax.random.normal(rng, extent, jnp.float32) * deviation
    if len(shards) > 0:
        entries = levels(rng, extent, shards, -0.22, 0.18) * entries
    return jnp.clip(entries, min=-limit, max=limit).astype(held_as)


def setup_inputs(seed: int = 0) -> dict:
    keys = jax.random.split(jax.random.key(seed), 9)
    return {
        "features": noise(keys[0], (BATCH * ROWS, C), 1.0, 6.0, ((0, 32),)),
        "timesteps": touch_ends(jax.random.randint(keys[1], (BATCH,), 0, 1000), jax.random.fold_in(keys[1], 1), 0, 999).astype(jnp.int32),
        "text_ids": touch_ends(ranked(keys[2], (BATCH, TEXT_LEN), VOCAB, 2), jax.random.fold_in(keys[2], 3), 0, VOCAB - 1).astype(jnp.int32),
        "text_table": noise(keys[3], (VOCAB, C), 2.0, 12.0, ((0, 512),)),
        "in_weights": noise(keys[4], (N_SEGMENT, C, C), C ** -0.5, 0.25, ((0, 16),)),
        "out_weights": noise(keys[5], (N_SEGMENT, C, C), C ** -0.5, 0.25, ((0, 16),)),
        "skip_weights": noise(keys[6], (N_SEGMENT, C, C), C ** -0.5, 0.25, ((0, 16),)),
        "cotangent": noise(keys[7], (BATCH * ROWS, C), ((MB * N_DP * ROWS) ** -0.5), 0.076171875, ((0, 32),)),
    }


EPSILON = 1e-05

def grouped(vector):
    lead = vector.shape[:-1]
    split = vector.reshape(lead + (GROUPS, vector.shape[-1] // GROUPS))
    total = lax.optimization_barrier(jnp.sum(split, axis=-1, keepdims=True))
    return jnp.broadcast_to(total, split.shape).reshape(vector.shape)

def normalize(block):
    group_size = block.shape[-2] * (block.shape[-1] // GROUPS)
    center = grouped(lax.optimization_barrier(jnp.sum(block, axis=-2, keepdims=True))) / group_size
    shifted = block - center
    spread = grouped(lax.optimization_barrier(jnp.sum(shifted * shifted, axis=-2, keepdims=True))) / group_size
    inv_scale = lax.rsqrt(spread + EPSILON)
    return (shifted * inv_scale, inv_scale)

def normalize_back(d_normed, normed, inv_scale):
    group_size = normed.shape[-2] * (normed.shape[-1] // GROUPS)
    mean_first = grouped(lax.optimization_barrier(jnp.sum(d_normed, axis=-2, keepdims=True))) / group_size
    mean_second = grouped(lax.optimization_barrier(jnp.sum(d_normed * normed, axis=-2, keepdims=True))) / group_size
    return inv_scale * (d_normed - mean_first - normed * mean_second)

def matmul(left, weight):
    in_shape = left.shape
    flattened = left.reshape(-1, in_shape[-1])
    product = jnp.dot(flattened, weight, preferred_element_type=jnp.float32)
    return product.reshape(in_shape[:-1] + (weight.shape[1],))

def matmul_transposed(left, weight):
    in_shape = left.shape
    flattened = left.reshape(-1, in_shape[-1])
    product = lax.dot_general(flattened, weight, (((1,), (1,)), ((), ())), preferred_element_type=jnp.float32)
    return product.reshape(in_shape[:-1] + (weight.shape[0],))

def swish_slope(pre_act):
    sigmoid_val = jax.nn.sigmoid(pre_act)
    return sigmoid_val * (1.0 + pre_act * (1.0 - sigmoid_val))

def encode_core(state_in, weight_in, weight_out, weight_skip, condition):
    current = state_in.astype(jnp.float32)
    normed, inv_scale = normalize(current)
    normed_low = normed.astype(jnp.bfloat16)
    pre_act = matmul(normed_low, weight_in) + condition
    hidden = jax.nn.silu(pre_act).astype(jnp.bfloat16)
    result = (current + matmul(hidden, weight_out)).astype(jnp.bfloat16)
    return (current, normed, inv_scale, normed_low, pre_act, hidden, result)

def encode(state_in, weight_in, weight_out, weight_skip, condition):
    parts = encode_core(state_in, weight_in, weight_out, weight_skip, condition)
    result = parts[6]
    skip_out = matmul(result, weight_skip).astype(jnp.bfloat16)
    return (result, skip_out)

def encode_back(state_in, weight_in, weight_out, weight_skip, condition, d_result, d_skip, weight_grad):
    current, normed, inv_scale, normed_low, pre_act, hidden, result = encode_core(state_in, weight_in, weight_out, weight_skip, condition)
    d_total = d_result.astype(jnp.float32) + matmul_transposed(d_skip, weight_skip)
    grad_skip = weight_grad(result, d_skip)
    d_total_low = d_total.astype(jnp.bfloat16)
    grad_out = weight_grad(hidden, d_total_low)
    d_act = (matmul_transposed(d_total_low, weight_out) * swish_slope(pre_act)).astype(jnp.bfloat16)
    grad_in = weight_grad(normed_low, d_act)
    d_normed = matmul_transposed(d_act, weight_in)
    d_inputs = (d_total + normalize_back(d_normed, normed, inv_scale)).astype(jnp.bfloat16)
    return (d_inputs, grad_in, grad_out, grad_skip)

def decode_core(state_in, skip_in, weight_in, weight_out, weight_skip, condition):
    current = state_in.astype(jnp.float32) + matmul(skip_in, weight_skip)
    normed, inv_scale = normalize(current)
    normed_low = normed.astype(jnp.bfloat16)
    pre_act = matmul(normed_low, weight_in) + condition
    hidden = jax.nn.silu(pre_act).astype(jnp.bfloat16)
    return (current, normed, inv_scale, normed_low, pre_act, hidden)

def decode(state_in, skip_in, weight_in, weight_out, weight_skip, condition):
    current, normed, inv_scale, normed_low, pre_act, hidden = decode_core(state_in, skip_in, weight_in, weight_out, weight_skip, condition)
    return (current + matmul(hidden, weight_out)).astype(jnp.bfloat16)

def decode_back(state_in, skip_in, weight_in, weight_out, weight_skip, condition, d_result, weight_grad):
    current, normed, inv_scale, normed_low, pre_act, hidden = decode_core(state_in, skip_in, weight_in, weight_out, weight_skip, condition)
    grad_out = weight_grad(hidden, d_result)
    d_act = (matmul_transposed(d_result, weight_out) * swish_slope(pre_act)).astype(jnp.bfloat16)
    grad_in = weight_grad(normed_low, d_act)
    d_normed = matmul_transposed(d_act, weight_in)
    d_current = (d_result.astype(jnp.float32) + normalize_back(d_normed, normed, inv_scale)).astype(jnp.bfloat16)
    grad_skip = weight_grad(skip_in, d_current)
    d_skip = matmul_transposed(d_current, weight_skip).astype(jnp.bfloat16)
    return (d_current, d_skip, grad_in, grad_out, grad_skip)

def time_embedding(steps, channels):
    half_width = channels // 2
    freqs = jnp.exp(-math.log(10000.0) * jnp.arange(half_width, dtype=jnp.float32) / half_width)
    angles = steps.astype(jnp.float32)[:, None] * freqs[None, :]
    return jnp.concatenate([jnp.cos(angles), jnp.sin(angles)], axis=-1)

def group_grad(left, right):
    left_groups = left.reshape(N_DP, -1, left.shape[-1]).astype(jnp.float32)
    right_groups = right.reshape(N_DP, -1, right.shape[-1]).astype(jnp.float32)
    return jnp.einsum('grc,grd->gcd', left_groups, right_groups, precision=lax.Precision.HIGHEST)

def finish(per_group):
    rounded = per_group.astype(jnp.bfloat16)
    rounded = lax.optimization_barrier(rounded)
    return lax.optimization_barrier(jnp.sum(rounded.astype(jnp.float32), axis=0))

def reference(features, timesteps, text_ids, text_table, in_weights, out_weights, skip_weights, cotangent):
    segments = in_weights.shape[0]
    half_segments = segments // 2
    batch_size = timesteps.shape[0]
    channels = features.shape[-1]
    pooled = lax.optimization_barrier(jnp.mean(jnp.take(text_table, text_ids, axis=0).astype(jnp.float32), axis=1))
    condition = (time_embedding(timesteps, channels) + pooled)[:, None, :]
    current = features.reshape(batch_size, -1, channels)
    inputs = []
    skip_list = []
    for section in range(half_segments):
        inputs.append(current)
        current, skip_out = encode(current, in_weights[section], out_weights[section], skip_weights[section], condition)
        skip_list.append(skip_out)
    for section in range(half_segments, segments):
        inputs.append(current)
        current = decode(current, skip_list[segments - 1 - section], in_weights[section], out_weights[section], skip_weights[section], condition)
    d_current = cotangent.reshape(batch_size, -1, channels)
    grad_in_list = [None] * segments
    grad_out_list = [None] * segments
    grad_skip_list = [None] * segments
    d_skips = [None] * half_segments
    for section in reversed(range(half_segments, segments)):
        d_current, d_skip, grad_in, grad_out, grad_skip = decode_back(inputs[section], skip_list[segments - 1 - section], in_weights[section], out_weights[section], skip_weights[section], condition, d_current, group_grad)
        d_skips[segments - 1 - section] = d_skip
        grad_in_list[section] = finish(grad_in)
        grad_out_list[section] = finish(grad_out)
        grad_skip_list[section] = finish(grad_skip)
    for section in reversed(range(half_segments)):
        d_current, grad_in, grad_out, grad_skip = encode_back(inputs[section], in_weights[section], out_weights[section], skip_weights[section], condition, d_current, d_skips[section], group_grad)
        grad_in_list[section] = finish(grad_in)
        grad_out_list[section] = finish(grad_out)
        grad_skip_list[section] = finish(grad_skip)
    return (jnp.stack(grad_in_list), jnp.stack(grad_out_list), jnp.stack(grad_skip_list))
```

```python
import math

import jax
import jax.numpy as jnp
from jax import lax
from jax.experimental import pallas as pl
from jax.experimental.pallas import tpu as pltpu
from jax.sharding import Mesh
from jax.sharding import PartitionSpec as P

C = 640
ROWS = 64
GROUPS = 32
MB = 3
NZ = 16
BF16 = jnp.bfloat16
F32 = jnp.float32
AXES = ("xh", "z", "y", "xl", "co")
DP = ("xh", "z")
SEG = ("y", "xl", "co")
MESH = pl.DeviceIdType.MESH
EPSILON = 1e-05


def dot(a, b):
    return jnp.dot(a, b, preferred_element_type=F32)


def dot_rhs_t(a, b):
    return lax.dot_general(a, b, (((1,), (1,)), ((), ())), preferred_element_type=F32)


def dot_lhs_t(a, b):
    return lax.dot_general(a, b, (((0,), (0,)), ((), ())), preferred_element_type=F32)


def iota(shape, dim):
    return lax.broadcasted_iota(jnp.int32, shape, dim)


def split(v, terms):
    out = []
    for _ in range(terms):
        part = v.astype(BF16)
        out.append(part)
        v = v - part.astype(F32)
    return out


def group_means(sums, terms, group_matrix):
    parts = [p for s in sums for p in split(s, terms)]
    pad = jnp.zeros((16 - len(parts), C), BF16)
    prod = dot(jnp.concatenate(parts + [pad], axis=0), group_matrix)
    out = []
    for k in range(len(sums)):
        total = prod[k * terms : k * terms + 1]
        for t in range(1, terms):
            total = total + prod[k * terms + t : k * terms + t + 1]
        out.append(total * (1.0 / (ROWS * (C // GROUPS))))
    return out


def normalize(v, group_matrix):
    (mean,) = group_means([jnp.sum(v, axis=0, keepdims=True)], 3, group_matrix)
    shifted = v - mean
    (var,) = group_means([jnp.sum(shifted * shifted, axis=0, keepdims=True)], 2, group_matrix)
    inv = lax.rsqrt(var + EPSILON)
    return shifted * inv, inv


def normalize_back(v, normed, inv, group_matrix):
    m1, m2 = group_means(
        [jnp.sum(v, axis=0, keepdims=True), jnp.sum(v * normed, axis=0, keepdims=True)],
        2,
        group_matrix,
    )
    return inv * (v - m1 - normed * m2)


def landed(ref, sem):
    pltpu.make_async_copy(ref, ref, sem).wait()


def kernel(
    feat,
    te,
    ids,
    table,
    w_in,
    w_out,
    w_skip,
    cot,
    out,
    W,
    cur,
    xbuf,
    dbuf,
    xin,
    din,
    xout,
    skout,
    L,
    R,
    sp,
    inv_std,
    LB,
    RB,
    gmat,
    s1m,
    s2m,
    p0f,
    p0b,
    c1,
    c2s,
    c2,
    c3s,
    c3,
    c4s,
    cnd,
    pm,
    pk,
    m_sp,
    m_rp,
    m_sm,
    m_rm,
    k_sp,
    k_rp,
    k_sm,
    k_rm,
    xe_s,
    xe_r,
    in_sem,
    wl,
    wcs,
    wcr,
    wxs,
    wxr,
    wfs,
    wfr,
    c1s_sem,
    c1r_sem,
    c2s_sem,
    c2r_sem,
    c3s_sem,
    c3r_sem,
    c4s_sem,
    c4r_sem,
    hop_s,
    hop_r,
    sk_s,
    sk_r,
    q_s,
    q_r,
    lp_s,
    lp_r,
    rp_s,
    rp_r,
    m_sps,
    m_rps,
    m_sms,
    m_rms,
    k_sps,
    k_rps,
    k_sms,
    k_rms,
    xe_sem,
):
    xh, z, y = lax.axis_index("xh"), lax.axis_index("z"), lax.axis_index("y")
    xl, co = lax.axis_index("xl"), lax.axis_index("co")
    j = xl * 2 + co
    p = xh * 4 + j
    weights = (w_in, w_out, w_skip)
    sample = jnp.minimum(j, MB - 1)
    worker = j < MB
    zc = 4 * j + y
    collector = z == zc
    yc, jc = z % 4, z // 4

    def remote(src, dst, ssem, rsem, dev):
        return pltpu.make_async_remote_copy(
            src_ref=src,
            dst_ref=dst,
            send_sem=ssem,
            recv_sem=rsem,
            device_id=dev,
            device_id_type=MESH,
        )

    for kind in range(3):
        pltpu.make_async_copy(weights[kind].at[0], W.at[kind, j], wl.at[kind]).start()
    rows = pl.ds(pl.multiple_of(sample * ROWS, ROWS), ROWS)
    pltpu.make_async_copy(feat.at[rows], xbuf, in_sem.at[0]).start()
    pltpu.make_async_copy(cot.at[rows], dbuf, in_sem.at[1]).start()

    barrier = pltpu.get_barrier_semaphore()

    def greet(dev):
        pl.semaphore_signal(barrier, inc=1, device_id=dev, device_id_type=MESH)

    for d in range(1, 8):
        q = (p + d) % 8
        greet((q // 4, z, y, (q // 2) % 2, q % 2))
    for d in range(1, 4):
        greet((xh, z, (y + d) % 4, xl, co))
    greet((xh, (z + 1) % NZ, y, xl, co))
    greet((xh, (z + NZ - 1) % NZ, y, xl, co))

    @pl.when(collector)
    def _():
        def tell(d, carry):
            greet((xh, (z + d) % NZ, y, xl, co))
            return carry

        lax.fori_loop(1, NZ, tell, 0)

    is_jc = j == jc
    is_yc = y == yc
    is_source = jnp.logical_and(is_jc, is_yc)

    @pl.when(jnp.logical_and(worker, jnp.logical_not(is_source)))
    def _():
        greet((xh, z, yc, jc // 2, jc % 2))

    base = ((((xh * NZ + z) * 4 + y) * 4) + j) * table.shape[0]
    tokens = ids[...] - base
    lane = iota((96, 128), 1)

    def count(v, acc):
        hits = jnp.sum(jnp.where(tokens == v, 1.0, 0.0), axis=1, keepdims=True)
        return jnp.where(lane == v, hits, acc)

    counts = lax.fori_loop(0, table.shape[0], count, jnp.zeros((96, 128), F32))
    r128 = iota((128, 96), 0)
    place = jnp.where(r128 % 4 < MB, (r128 // 4) * MB + r128 % 4, -1)
    spread = jnp.where(place == iota((128, 96), 1), 1.0, 0.0).astype(BF16)
    counts = dot(spread, counts.astype(BF16))[:, : table.shape[0]].astype(BF16)
    part = dot(counts, table[...]) * (1.0 / ids.shape[1])
    p0f[...] = part.reshape(8, 16, C)
    p0b[...] = p0f[...].astype(BF16)

    expect = 12 + jnp.where(
        collector, 12 - jnp.where(worker, 1, 0), 1
    )
    pl.semaphore_wait(barrier, expect)

    core_dev = (xh, z, y, xl, 1 - co)
    x_devs = ((xh, z, y, 1 - xl, co), (1 - xh, z, y, 1 - xl, co))
    halves = (pl.ds(0, C // 2), pl.ds(C // 2, C // 2))
    far = 2 * (1 - xl) + co

    def start_weights(kind):
        for h in range(2):
            remote(
                weights[kind].at[0, halves[h]],
                W.at[kind, j, halves[h]],
                wxs.at[kind, h],
                wxr.at[kind, h],
                x_devs[h],
            ).start()
        remote(
            weights[kind].at[0], W.at[kind, j], wcs.at[kind], wcr.at[kind], core_dev
        ).start()

    def relay_weights(kind):
        for h in range(2):
            block = W.at[kind, far, halves[h]]
            landed(block, wxr.at[kind, h])
            remote(block, block, wfs.at[kind, h], wfr.at[kind, h], core_dev).start()

    def wait_weights(kind):
        landed(W.at[kind, 0], wl.at[kind])
        landed(W.at[kind, 0], wcr.at[kind])
        for h in range(2):
            landed(W.at[kind, 0, halves[h]], wfr.at[kind, h])

    for d in range(1, 8):
        q = (p + d) % 8
        remote(
            p0b.at[q],
            c1.at[p],
            c1s_sem.at[d],
            c1r_sem.at[p],
            (q // 4, z, y, (q // 2) % 2, q % 2),
        ).start()
    start_weights(0)
    start_weights(1)

    gmat[...] = jnp.where(
        iota((C, 1), 0) // (C // GROUPS) == iota((1, C), 1) // (C // GROUPS), 1.0, 0.0
    ).astype(BF16)
    col = iota((1, C), 1)
    src1 = (col % 40) // 20 * 320 + (col // 40) * 20 + col % 20
    s1m[...] = jnp.where(iota((C, 1), 0) == src1, 1.0, 0.0).astype(BF16)
    col = iota((1, 768), 1)
    off = col % 48
    src2 = jnp.where(off < 40, off // 20 * 320 + (col // 48) * 20 + off % 20, -1)
    s2m[...] = jnp.where(iota((C, 1), 0) == src2, 1.0, 0.0).astype(BF16)

    acc = p0f[p]
    for d in range(1, 8):
        q = (p + d) % 8
        landed(c1.at[q], c1r_sem.at[q])
        acc = acc + c1[q].astype(F32)
    c2s[...] = acc.astype(BF16)
    for d in range(1, 4):
        remote(
            c2s, c2.at[y], c2s_sem.at[d], c2r_sem.at[y], (xh, z, (y + d) % 4, xl, co)
        ).start()
    for d in range(1, 4):
        q = (y + d) % 4
        landed(c2.at[q], c2r_sem.at[q])
        acc = acc + c2[q].astype(F32)

    @pl.when(jnp.logical_not(collector))
    def _():
        c3s[...] = acc.astype(BF16)
        remote(c3s, c3.at[z], c3s_sem, c3r_sem.at[z], (xh, zc, y, xl, co)).start()

    @pl.when(collector)
    def _():
        def gather(d, total):
            q = (z + d) % NZ
            landed(c3.at[q], c3r_sem.at[q])
            return total + c3[q].astype(F32)

        total = lax.fori_loop(1, NZ, gather, acc)
        row = iota((16, C), 0)
        picked = [
            jnp.sum(jnp.where(row == 4 * y + m, total, 0.0), axis=0, keepdims=True)
            for m in range(MB)
        ]
        c4s[...] = jnp.concatenate(picked + [jnp.zeros((8 - MB, C), F32)], axis=0)

        def give(q, carry):
            qy, qj = q // MB, q % MB

            @pl.when(jnp.logical_not(jnp.logical_and(qy == y, qj == j)))
            def _():
                remote(
                    c4s, cnd, c4s_sem.at[q], c4r_sem, (xh, z, qy, qj // 2, qj % 2)
                ).start()

            return carry

        lax.fori_loop(0, 4 * MB, give, 0)

        @pl.when(worker)
        def _():
            cnd[...] = c4s[...]

    start_weights(2)

    @pl.when(jnp.logical_and(worker, jnp.logical_not(is_source)))
    def _():
        landed(cnd, c4r_sem)

    relay_weights(0)
    relay_weights(1)
    wait_weights(0)
    wait_weights(1)
    landed(xbuf, in_sem.at[0])
    landed(dbuf, in_sem.at[1])

    def condition():
        both = cnd[...] + te[...]
        return jnp.sum(
            jnp.where(iota((8, C), 0) == j, both, 0.0), axis=0, keepdims=True
        )

    def activate(i, v, cond):
        normed, inv = normalize(v, gmat[...])
        low = normed.astype(BF16)
        L[i, 0] = low
        inv_std[i] = jnp.broadcast_to(inv, (8, C))
        act = dot(low, W[0, i]) + cond
        sig = 1.0 / (1.0 + jnp.exp(-act))
        hidden = (act * sig).astype(BF16)
        L[i, 1] = hidden
        sp[i] = sig * (1.0 + act * (1.0 - sig))
        return (v + dot(hidden, W[1, i])).astype(BF16)

    def back(i, d_low, d_full):
        R[i, 1] = d_low
        e = (dot_rhs_t(d_low, W[1, i]) * sp[i]).astype(BF16)
        R[i, 0] = e
        v = dot_rhs_t(e, W[0, i])
        g = normalize_back(v, L[i, 0].astype(F32), inv_std[i, 0:1], gmat[...])
        return (d_full + g).astype(BF16)

    def send_part(buf, i, dst, ssem, rsem):
        @pl.when(i == j)
        def _():
            pltpu.make_async_copy(buf.at[i], dst.at[sample], rsem.at[sample]).start()

        @pl.when(i != j)
        def _():
            remote(
                buf.at[i],
                dst.at[sample],
                ssem.at[i],
                rsem.at[sample],
                (xh, z, y, i // 2, i % 2),
            ).start()

    def done_part(buf, ssem):
        def one(i, carry):
            @pl.when(i != j)
            def _():
                landed(buf.at[i], ssem.at[i])

            return carry

        lax.fori_loop(0, 4, one, 0)

    up = (xh, z, (y + 1) % 4, xl, co)
    down = (xh, z, (y + 3) % 4, xl, co)
    across = (xh, z, 3 - y, xl, co)
    encoder = y < 2

    @pl.when(encoder)
    def _():
        @pl.when(worker)
        def _():
            cond = condition()

            @pl.when(y == 0)
            def _():
                cur[...] = xbuf[...].astype(F32)

            @pl.when(y == 1)
            def _():
                landed(xin, hop_r.at[0])
                cur[...] = xin[...].astype(F32)

            def step(i, carry):
                result = activate(i, cur[...], cond)
                L[i, 2] = result
                cur[...] = result.astype(F32)
                return carry

            lax.fori_loop(0, 4, step, 0)
            remote(L.at[3, 2], xin, hop_s.at[0], hop_r.at[0], up).start()

        relay_weights(2)
        wait_weights(2)

        @pl.when(worker)
        def _():
            def give_skip(n, carry):
                i = 3 - n
                skout[i] = dot(L[i, 2], W[2, i]).astype(BF16)
                remote(
                    skout.at[i], L.at[3 - i, 2], sk_s.at[i], sk_r.at[3 - i], across
                ).start()
                return carry

            lax.fori_loop(0, 4, give_skip, 0)

            def give_left(i, carry):
                send_part(L, i, LB, lp_s, lp_r)
                return carry

            lax.fori_loop(0, 4, give_left, 0)

            landed(din, hop_r.at[1])
            cur[...] = din[...].astype(F32)

            def step_back(n, carry):
                i = 3 - n
                landed(R.at[i, 2], q_r.at[i])
                d_full = cur[...] + dot_rhs_t(R[i, 2], W[2, i])
                d_low = back(i, d_full.astype(BF16), d_full)
                cur[...] = d_low.astype(F32)
                send_part(R, i, RB, rp_s, rp_r)
                return carry

            lax.fori_loop(0, 4, step_back, 0)

            @pl.when(y == 1)
            def _():
                xout[...] = cur[...].astype(BF16)
                remote(xout, din, hop_s.at[1], hop_r.at[1], down).start()

            landed(L.at[3, 2], hop_s.at[0])

            def finish(i, carry):
                landed(skout.at[i], sk_s.at[i])
                return carry

            lax.fori_loop(0, 4, finish, 0)

            @pl.when(y == 1)
            def _():
                landed(xout, hop_s.at[1])

    @pl.when(jnp.logical_not(encoder))
    def _():
        relay_weights(2)
        wait_weights(2)

        @pl.when(worker)
        def _():
            cond = condition()
            landed(xin, hop_r.at[0])
            cur[...] = xin[...].astype(F32)

            def step(i, carry):
                landed(L.at[i, 2], sk_r.at[i])
                v = cur[...] + dot(L[i, 2], W[2, i])
                cur[...] = activate(i, v, cond).astype(F32)
                return carry

            lax.fori_loop(0, 4, step, 0)

            @pl.when(y == 2)
            def _():
                xout[...] = cur[...].astype(BF16)
                remote(xout, xin, hop_s.at[0], hop_r.at[0], up).start()

            def give_left(i, carry):
                send_part(L, i, LB, lp_s, lp_r)
                return carry

            lax.fori_loop(0, 4, give_left, 0)

            @pl.when(y == 3)
            def _():
                cur[...] = dbuf[...].astype(F32)

            @pl.when(y == 2)
            def _():
                landed(din, hop_r.at[1])
                cur[...] = din[...].astype(F32)

            def step_back(n, carry):
                i = 3 - n
                d_full = cur[...]
                g = back(i, d_full.astype(BF16), d_full)
                R[i, 2] = g
                cur[...] = g.astype(F32)
                send_part(R, i, RB, rp_s, rp_r)
                return carry

            lax.fori_loop(0, 4, step_back, 0)
            remote(R.at[0, 2], din, hop_s.at[1], hop_r.at[1], down).start()

            def give_q(i, carry):
                skout[i] = dot_rhs_t(R[i, 2], W[2, i]).astype(BF16)
                remote(
                    skout.at[i], R.at[3 - i, 2], q_s.at[i], q_r.at[3 - i], across
                ).start()
                return carry

            lax.fori_loop(0, 4, give_q, 0)
            landed(R.at[0, 2], hop_s.at[1])

            def finish(i, carry):
                landed(skout.at[i], q_s.at[i])
                return carry

            lax.fori_loop(0, 4, finish, 0)

            @pl.when(y == 2)
            def _():
                landed(xout, hop_s.at[0])

    for m in range(MB):
        landed(LB.at[m], lp_r.at[m])
    for m in range(MB):
        landed(RB.at[m], rp_r.at[m])

    def stacked(ref, kind):
        return jnp.concatenate([ref[m, kind] for m in range(MB)], axis=0)

    left = dot(stacked(LB, 2), s2m[...]).astype(BF16)
    grad = dot_lhs_t(left, stacked(RB, 2))
    for c in range(NZ):
        pk[c] = grad[48 * c : 48 * c + 48]
    for kind in range(2):
        left = dot(stacked(LB, kind), s1m[...]).astype(BF16)
        grad = dot_lhs_t(left, stacked(RB, kind))
        for c in range(NZ):
            pm[c, 40 * kind : 40 * kind + 40] = grad[40 * c : 40 * c + 40]

    after = (xh, (z + 1) % NZ, y, xl, co)
    before = (xh, (z + NZ - 1) % NZ, y, xl, co)
    rings = (
        (pk, k_sp, k_rp, k_sm, k_rm, k_sps, k_rps, k_sms, k_rms),
        (pm, m_sp, m_rp, m_sm, m_rm, m_sps, m_rps, m_sms, m_rms),
    )
    half = NZ // 2

    def plus(ring, t, first):
        own, sbuf, rbuf, _, _, ssem, rsem, _, _ = ring
        total = own[(z + half - t + NZ) % NZ]
        if not first:
            landed(rbuf.at[t - 1], rsem.at[t - 1])
            total = total + rbuf[t - 1].astype(F32)
        sbuf[t] = total.astype(BF16)
        remote(sbuf.at[t], rbuf.at[t], ssem.at[t], rsem.at[t], after).start()

    def minus(ring, t, first):
        own, _, _, sbuf, rbuf, _, _, ssem, rsem = ring
        total = own[(z - half + 1 + t + NZ) % NZ]
        if not first:
            landed(rbuf.at[t - 1], rsem.at[t - 1])
            total = total + rbuf[t - 1].astype(F32)
        sbuf[t] = total.astype(BF16)
        remote(sbuf.at[t], rbuf.at[t], ssem.at[t], rsem.at[t], before).start()

    for ring in rings:
        plus(ring, 0, True)
        minus(ring, 0, True)

    def ring_step(t, carry):
        for ring in rings:
            plus(ring, t, False)
            minus(ring, t, False)
        return carry

    lax.fori_loop(1, half - 1, ring_step, 0)
    for ring in rings:
        plus(ring, half - 1, False)
    totals = []
    for ring in rings:
        own, _, rp, _, rm, _, rps, _, rms = ring
        landed(rp.at[half - 1], rps.at[half - 1])
        landed(rm.at[half - 2], rms.at[half - 2])
        totals.append(own[z] + rp[half - 1].astype(F32) + rm[half - 2].astype(F32))

    total = jnp.concatenate([totals[1], totals[0]], axis=0)
    r = iota((64, 128), 0)
    start = r // 20 * 40 + r % 20

    def choose(side):
        source = jnp.where(r < 60, start + 20 * side, -1)
        return jnp.where(source == iota((64, 128), 1), 1.0, 0.0).astype(BF16)

    xe_s[...] = dot(choose(1 - xh), total.astype(BF16)).astype(BF16)
    exchange = remote(
        xe_s, xe_r, xe_sem.at[0], xe_sem.at[1], (1 - xh, z, y, xl, co)
    )
    exchange.start()
    mine = choose(xh)
    own = sum(dot(mine, piece) for piece in split(total, 2))
    exchange.wait_recv()
    out[...] = own + xe_r[...].astype(F32)

    exchange.wait_send()
    for d in range(1, 8):
        landed(p0b.at[0], c1s_sem.at[d])
    for d in range(1, 4):
        landed(c2s, c2s_sem.at[d])

    @pl.when(jnp.logical_not(collector))
    def _():
        landed(c3s, c3s_sem)

    @pl.when(collector)
    def _():
        def given(q, carry):
            qy, qj = q // MB, q % MB

            @pl.when(jnp.logical_not(jnp.logical_and(qy == y, qj == j)))
            def _():
                landed(c4s, c4s_sem.at[q])

            return carry

        lax.fori_loop(0, 4 * MB, given, 0)

    for kind in range(3):
        landed(W.at[kind, 0], wcs.at[kind])
        for h in range(2):
            landed(W.at[kind, 0, halves[h]], wxs.at[kind, h])
            landed(W.at[kind, 0, halves[h]], wfs.at[kind, h])

    @pl.when(worker)
    def _():
        done_part(L, lp_s)
        done_part(R, rp_s)

    def left_ring(t, carry):
        landed(k_sp.at[t], k_sps.at[t])
        landed(m_sp.at[t], m_sps.at[t])
        return carry

    lax.fori_loop(0, half, left_ring, 0)

    def left_ring_back(t, carry):
        landed(k_sm.at[t], k_sms.at[t])
        landed(m_sm.at[t], m_sms.at[t])
        return carry

    lax.fori_loop(0, half - 1, left_ring_back, 0)


def time_embedding(steps, channels):
    half_width = channels // 2
    freqs = jnp.exp(-math.log(10000.0) * jnp.arange(half_width, dtype=F32) / half_width)
    angles = steps.astype(F32)[:, None] * freqs[None, :]
    return jnp.concatenate([jnp.cos(angles), jnp.sin(angles)], axis=-1)


def on_device(features, timesteps, text_ids, text_table, w_in, w_out, w_skip, cotangent):
    te = jnp.pad(time_embedding(timesteps, C), ((0, 8 - MB), (0, 0)))
    dma = pltpu.SemaphoreType.DMA
    half = NZ // 2

    def bf(*shape):
        return pltpu.VMEM(shape, BF16)

    def f32(*shape):
        return pltpu.VMEM(shape, F32)

    block = (ROWS, C)
    scratch = [
        bf(3, 4, C, C),
        f32(*block),
        bf(*block),
        bf(*block),
        bf(*block),
        bf(*block),
        bf(*block),
        bf(4, *block),
        bf(4, 3, *block),
        bf(4, 3, *block),
        f32(4, *block),
        f32(4, 8, C),
        bf(MB, 3, *block),
        bf(MB, 3, *block),
        bf(C, C),
        bf(C, C),
        bf(C, 768),
        f32(8, 16, C),
        bf(8, 16, C),
        bf(8, 16, C),
        bf(16, C),
        bf(4, 16, C),
        bf(16, C),
        bf(NZ, 16, C),
        f32(8, C),
        f32(8, C),
        f32(NZ, 80, C),
        f32(NZ, 48, C),
        bf(half, 80, C),
        bf(half, 80, C),
        bf(half - 1, 80, C),
        bf(half - 1, 80, C),
        bf(half, 48, C),
        bf(half, 48, C),
        bf(half - 1, 48, C),
        bf(half - 1, 48, C),
        bf(64, C),
        bf(64, C),
        dma((2,)),
        dma((3,)),
        dma((3,)),
        dma((3,)),
        dma((3, 2)),
        dma((3, 2)),
        dma((3, 2)),
        dma((3, 2)),
        dma((8,)),
        dma((8,)),
        dma((4,)),
        dma((4,)),
        dma,
        dma((NZ,)),
        dma((4 * MB,)),
        dma,
        dma((2,)),
        dma((2,)),
        dma((4,)),
        dma((4,)),
        dma((4,)),
        dma((4,)),
        dma((4,)),
        dma((MB,)),
        dma((4,)),
        dma((MB,)),
        dma((half,)),
        dma((half,)),
        dma((half - 1,)),
        dma((half - 1,)),
        dma((half,)),
        dma((half,)),
        dma((half - 1,)),
        dma((half - 1,)),
        dma((2,)),
    ]
    vmem = pl.BlockSpec(memory_space=pltpu.VMEM)
    hbm = pl.BlockSpec(memory_space=pl.ANY)
    grads = pl.pallas_call(
        kernel,
        out_shape=jax.ShapeDtypeStruct((64, C), F32),
        in_specs=[hbm, vmem, vmem, vmem, hbm, hbm, hbm, hbm],
        out_specs=vmem,
        scratch_shapes=scratch,
        compiler_params=pltpu.CompilerParams(
            collective_id=0, has_side_effects=True, vmem_limit_bytes=56 * 2**20
        ),
        name="unet_step",
    )(features, te, text_ids, text_table, w_in, w_out, w_skip, cotangent)
    return tuple(grads[None, 20 * k : 20 * k + 20] for k in range(3))


def solution(mesh):
    split_mesh = Mesh(mesh.devices.reshape(2, NZ, 4, 2, 2), AXES)
    weight = P(SEG, None, None)
    return jax.shard_map(
        on_device,
        mesh=split_mesh,
        in_specs=(
            P(DP, None),
            P(DP),
            P(),
            P(DP + SEG, None),
            weight,
            weight,
            weight,
            P(DP, None),
        ),
        out_specs=(P(SEG, DP, None),) * 3,
        check_vma=False,
    )
```

```python
import math

import jax
import jax.numpy as jnp
from jax import lax
from jax.experimental import pallas as pl
from jax.experimental.pallas import tpu as pltpu
from jax.sharding import Mesh
from jax.sharding import PartitionSpec as P

C = 640
ROWS = 64
GROUPS = 32
MB = 3
NZ = 16
BF16 = jnp.bfloat16
F32 = jnp.float32
AXES = ("xh", "z", "y", "xl", "co")
DP = ("xh", "z")
SEG = ("y", "xl", "co")
MESH = pl.DeviceIdType.MESH
EPSILON = 1e-05


def dot(a, b):
    return jnp.dot(a, b, preferred_element_type=F32)


def dot_rhs_t(a, b):
    return lax.dot_general(a, b, (((1,), (1,)), ((), ())), preferred_element_type=F32)


def dot_lhs_t(a, b):
    return lax.dot_general(a, b, (((0,), (0,)), ((), ())), preferred_element_type=F32)


def iota(shape, dim):
    return lax.broadcasted_iota(jnp.int32, shape, dim)


def split(v, terms):
    out = []
    for _ in range(terms):
        part = v.astype(BF16)
        out.append(part)
        v = v - part.astype(F32)
    return out


def group_means(sums, terms, group_matrix):
    parts = [p for s in sums for p in split(s, terms)]
    pad = jnp.zeros((16 - len(parts), C), BF16)
    prod = dot(jnp.concatenate(parts + [pad], axis=0), group_matrix)
    out = []
    for k in range(len(sums)):
        total = prod[k * terms : k * terms + 1]
        for t in range(1, terms):
            total = total + prod[k * terms + t : k * terms + t + 1]
        out.append(total * (1.0 / (ROWS * (C // GROUPS))))
    return out


def normalize(v, group_matrix):
    (mean,) = group_means([jnp.sum(v, axis=0, keepdims=True)], 3, group_matrix)
    shifted = v - mean
    (var,) = group_means([jnp.sum(shifted * shifted, axis=0, keepdims=True)], 2, group_matrix)
    inv = lax.rsqrt(var + EPSILON)
    return shifted * inv, inv


def normalize_back(v, normed, inv, group_matrix):
    m1, m2 = group_means(
        [jnp.sum(v, axis=0, keepdims=True), jnp.sum(v * normed, axis=0, keepdims=True)],
        2,
        group_matrix,
    )
    return inv * (v - m1 - normed * m2)


def landed(ref, sem):
    pltpu.make_async_copy(ref, ref, sem).wait()


def kernel(
    steps,
    feat,
    ids_in,
    table_in,
    w_in,
    w_out,
    w_skip,
    cot,
    out_a,
    out_b,
    ids,
    table,
    W,
    cur,
    xbuf,
    dbuf,
    xin,
    din,
    xout,
    skout,
    pre,
    L,
    R,
    sp,
    inv_std,
    LB,
    RB,
    LP,
    gmat,
    s_low,
    s_high,
    p0f,
    p0b,
    c1,
    c2s,
    c2,
    c3s,
    c3,
    pm,
    sbp,
    rbp,
    sbm,
    rbm,
    lastp,
    lastm,
    cross,
    fin,
    in_sem,
    wl,
    wcs,
    wcr,
    wxs,
    wxr,
    wfs,
    wfr,
    c1s_sem,
    c1r_sem,
    c2s_sem,
    c2r_sem,
    c3s_sem,
    c3r_sem,
    hop_s,
    hop_r,
    sk_s,
    sk_r,
    q_s,
    q_r,
    lp_s,
    lp_r,
    rp_s,
    rp_r,
    sps,
    rps,
    sms,
    rms,
    fin_s,
    fin_r,
):
    xh, z, y = lax.axis_index("xh"), lax.axis_index("z"), lax.axis_index("y")
    xl, co = lax.axis_index("xl"), lax.axis_index("co")
    j = xl * 2 + co
    p = xh * 4 + j
    weights = (w_in, w_out, w_skip)
    sample = jnp.minimum(j, MB - 1)
    worker = j < MB
    def remote(src, dst, ssem, rsem, dev):
        return pltpu.make_async_remote_copy(
            src_ref=src,
            dst_ref=dst,
            send_sem=ssem,
            recv_sem=rsem,
            device_id=dev,
            device_id_type=MESH,
        )

    for kind in range(3):
        pltpu.make_async_copy(weights[kind].at[0], W.at[kind, j], wl.at[kind]).start()
    pltpu.make_async_copy(ids_in, ids, in_sem.at[2]).start()
    pltpu.make_async_copy(table_in, table, in_sem.at[3]).start()
    rows = pl.ds(pl.multiple_of(sample * ROWS, ROWS), ROWS)
    pltpu.make_async_copy(feat.at[rows], xbuf, in_sem.at[0]).start()
    pltpu.make_async_copy(cot.at[rows], dbuf, in_sem.at[1]).start()

    barrier = pltpu.get_barrier_semaphore()

    def greet(dev):
        pl.semaphore_signal(barrier, inc=1, device_id=dev, device_id_type=MESH)

    for d in range(1, 8):
        q = (p + d) % 8
        greet((q // 4, z, y, (q // 2) % 2, q % 2))
    for d in range(1, 4):
        greet((xh, z, (y + d) % 4, xl, co))
    for side in (1, NZ - 1):
        greet((1 - xh, (z + side) % NZ, y, xl, co))

    def greet_z(d, carry):
        greet((xh, (z + d) % NZ, y, xl, co))
        return carry

    lax.fori_loop(1, NZ, greet_z, 0)

    landed(ids, in_sem.at[2])
    landed(table, in_sem.at[3])
    base = ((((xh * NZ + z) * 4 + y) * 4) + j) * table.shape[0]
    tokens = ids[...] - base
    words = table.shape[0]
    row = iota((words, 96), 0)

    def count(n, acc):
        for u in range(8):
            v = n * 8 + u
            hits = jnp.sum(jnp.where(tokens == v, 1.0, 0.0), axis=0, keepdims=True)
            acc = jnp.where(row == v, hits, acc)
        return acc

    counts = lax.fori_loop(0, words // 8, count, jnp.zeros((words, 96), F32))
    r96 = iota((1, 96), 1)
    place = (r96 // 48) * 48 + (r96 % 16) * MB + (r96 % 48) // 16
    order = jnp.where(place == iota((96, 1), 0), 1.0, 0.0).astype(BF16)
    counts = dot(counts.astype(BF16), order).astype(BF16)
    part = dot_lhs_t(counts, table[...]) * (1.0 / ids.shape[0])
    p0f[...] = part.reshape(2 * MB, 16, C)
    p0b[...] = p0f[...].astype(BF16)

    pl.semaphore_wait(barrier, 7 + 3 + 2 + NZ - 1)

    core_dev = (xh, z, y, xl, 1 - co)
    x_devs = ((xh, z, y, 1 - xl, co), (1 - xh, z, y, 1 - xl, co))
    halves = (pl.ds(0, C // 2), pl.ds(C // 2, C // 2))
    far = 2 * (1 - xl) + co

    def start_weights(kind):
        for h in range(2):
            remote(
                weights[kind].at[0, halves[h]],
                W.at[kind, j, halves[h]],
                wxs.at[kind, h],
                wxr.at[kind, h],
                x_devs[h],
            ).start()
        remote(
            weights[kind].at[0], W.at[kind, j], wcs.at[kind], wcr.at[kind], core_dev
        ).start()

    def relay_weights(kind):
        for h in range(2):
            block = W.at[kind, far, halves[h]]
            landed(block, wxr.at[kind, h])
            remote(block, block, wfs.at[kind, h], wfr.at[kind, h], core_dev).start()

    def wait_weights(kind):
        landed(W.at[kind, 0], wl.at[kind])
        landed(W.at[kind, 0], wcr.at[kind])
        for h in range(2):
            landed(W.at[kind, 0, halves[h]], wfr.at[kind, h])

    for b in range(2 * MB):
        bx, bj = b // MB, b % MB

        @pl.when(p != 4 * bx + bj)
        def _():
            remote(
                p0b.at[b],
                c1.at[p],
                c1s_sem.at[b],
                c1r_sem.at[p],
                (bx, z, y, bj // 2, bj % 2),
            ).start()

    start_weights(0)
    start_weights(1)
    gmat[...] = jnp.where(
        iota((C, 1), 0) // (C // GROUPS) == iota((1, C), 1) // (C // GROUPS), 1.0, 0.0
    ).astype(BF16)

    @pl.when(worker)
    def _():
        acc = p0f[xh * MB + sample]
        for d in range(1, 8):
            q = (p + d) % 8
            landed(c1.at[q], c1r_sem.at[q])
            acc = acc + c1[q].astype(F32)
        c2s[...] = acc.astype(BF16)
        for d in range(1, 4):
            remote(
                c2s, c2.at[y], c2s_sem.at[d], c2r_sem.at[y], (xh, z, (y + d) % 4, xl, co)
            ).start()
        for d in range(1, 4):
            q = (y + d) % 4
            landed(c2.at[q], c2r_sem.at[q])
            acc = acc + c2[q].astype(F32)
        for r in range(NZ):
            c3s[r] = acc[r : r + 1]

        def give(d, carry):
            q = (z + d) % NZ
            remote(
                c3s.at[q], c3.at[z], c3s_sem.at[q], c3r_sem.at[z], (xh, q, y, xl, co)
            ).start()
            return carry

        lax.fori_loop(1, NZ, give, 0)

    start_weights(2)
    relay_weights(0)
    relay_weights(1)

    @pl.when(y > 0)
    def _():
        relay_weights(2)

    landed(xbuf, in_sem.at[0])
    landed(dbuf, in_sem.at[1])

    def condition():
        lane = iota((1, C), 1)
        half_width = C // 2
        k = jnp.where(lane < half_width, lane, lane - half_width).astype(F32)
        freqs = jnp.exp(-math.log(10000.0) * k / half_width)
        angles = steps[sample].astype(F32) * freqs
        total = jnp.where(lane < half_width, jnp.cos(angles), jnp.sin(angles)) + c3s[z]

        def add(d, acc):
            q = (z + d) % NZ
            landed(c3.at[q], c3r_sem.at[q])
            return acc + c3[q]

        return lax.fori_loop(1, NZ, add, total)


    def startup_sent():
        for b in range(2 * MB):
            bx, bj = b // MB, b % MB

            @pl.when(p != 4 * bx + bj)
            def _():
                landed(p0b.at[0], c1s_sem.at[b])

        @pl.when(worker)
        def _():
            for d in range(1, 4):
                landed(c2s, c2s_sem.at[d])

            def given(d, carry):
                q = (z + d) % NZ
                landed(c3s.at[q], c3s_sem.at[q])
                return carry

            lax.fori_loop(1, NZ, given, 0)

        for kind in range(3):
            landed(W.at[kind, 0], wcs.at[kind])
            for h in range(2):
                landed(W.at[kind, 0, halves[h]], wxs.at[kind, h])
                landed(W.at[kind, 0, halves[h]], wfs.at[kind, h])

    def chain_sent():
        startup_sent()

        @pl.when(worker)
        def _():
            done_part(L, lp_s)
            done_part(R, rp_s)

            def sent(i, carry):
                @pl.when(encoder)
                def _():
                    landed(skout.at[i], sk_s.at[i])

                @pl.when(jnp.logical_not(encoder))
                def _():
                    landed(skout.at[i], q_s.at[i])

                return carry

            lax.fori_loop(0, 4, sent, 0)

            @pl.when(y < 3)
            def _():
                landed(xout, hop_s.at[0])

            @pl.when(y > 0)
            def _():
                landed(xout, hop_s.at[1])

    def activate(i, v, cond):
        normed, inv = normalize(v, gmat[...])
        low = normed.astype(BF16)
        L[i, 0] = low
        inv_std[i] = jnp.broadcast_to(inv, (8, C))
        act = dot(low, W[0, i]) + cond
        sig = 1.0 / (1.0 + jnp.exp(-act))
        hidden = (act * sig).astype(BF16)
        L[i, 1] = hidden
        sp[i] = sig * (1.0 + act * (1.0 - sig))
        return (v + dot(hidden, W[1, i])).astype(BF16)

    def back(i, d_low, d_full):
        R[i, 1] = d_low
        e = (dot_rhs_t(d_low, W[1, i]) * sp[i]).astype(BF16)
        R[i, 0] = e
        v = dot_rhs_t(e, W[0, i])
        g = normalize_back(v, L[i, 0].astype(F32), inv_std[i, 0:1], gmat[...])
        return (d_full + g).astype(BF16)

    def send_part(buf, i, dst, ssem, rsem):
        @pl.when(i == j)
        def _():
            pltpu.make_async_copy(buf.at[i], dst.at[sample], rsem.at[sample]).start()

        @pl.when(i != j)
        def _():
            remote(
                buf.at[i],
                dst.at[sample],
                ssem.at[i],
                rsem.at[sample],
                (xh, z, y, i // 2, i % 2),
            ).start()

    def done_part(buf, ssem):
        def one(i, carry):
            @pl.when(i != j)
            def _():
                landed(buf.at[i], ssem.at[i])

            return carry

        lax.fori_loop(0, 4, one, 0)

    up = (xh, z, (y + 1) % 4, xl, co)
    down = (xh, z, (y + 3) % 4, xl, co)
    across = (xh, z, 3 - y, xl, co)
    encoder = y < 2

    def give_left():
        def one(i, carry):
            send_part(L, i, LB, lp_s, lp_r)
            return carry

        lax.fori_loop(0, 4, one, 0)

    def stacked(ref, kind):
        return jnp.concatenate([ref[m, kind] for m in range(MB)], axis=0)

    def order_left():
        col = iota((1, 2 * NZ * 24), 1)
        block, off = col // 24, col % 24
        first = (block % 2) * (C // 2) + (block // 2) * 20
        row = iota((C, 1), 0)
        low = jnp.where(off < 20, first + off, -1)
        high = jnp.where(off >= 4, first + off - 4, -1)
        s_low[...] = jnp.where(row == low, 1.0, 0.0).astype(BF16)
        s_high[...] = jnp.where(row == high, 1.0, 0.0).astype(BF16)
        for m in range(MB):
            landed(LB.at[m], lp_r.at[m])
        LP[0] = dot(stacked(LB, 0), s_low[...]).astype(BF16)
        LP[1] = dot(stacked(LB, 1), s_high[...]).astype(BF16)
        LP[2] = dot(stacked(LB, 2), s_low[...]).astype(BF16)

    @pl.when(encoder)
    def _():
        @pl.when(worker)
        def _():
            cond = condition()
            wait_weights(0)
            wait_weights(1)

            @pl.when(y == 0)
            def _():
                cur[...] = xbuf[...].astype(F32)

            @pl.when(y == 1)
            def _():
                landed(xin, hop_r.at[0])
                cur[...] = xin[...].astype(F32)

            def step(i, carry):
                result = activate(i, cur[...], cond)
                L[i, 2] = result
                cur[...] = result.astype(F32)
                return carry

            lax.fori_loop(0, 4, step, 0)
            remote(L.at[3, 2], xin, hop_s.at[0], hop_r.at[0], up).start()

        @pl.when(jnp.logical_not(worker))
        def _():
            wait_weights(0)
            wait_weights(1)

        @pl.when(y == 0)
        def _():
            relay_weights(2)

        wait_weights(2)

        @pl.when(worker)
        def _():
            def give_skip(n, carry):
                i = 3 - n
                skout[i] = dot(L[i, 2], W[2, i]).astype(BF16)
                remote(
                    skout.at[i], L.at[3 - i, 2], sk_s.at[i], sk_r.at[3 - i], across
                ).start()
                return carry

            lax.fori_loop(0, 4, give_skip, 0)
            give_left()

        order_left()

        @pl.when(worker)
        def _():
            def skip_back(i):
                landed(R.at[i, 2], q_r.at[i])
                pre[i] = dot_rhs_t(R[i, 2], W[2, i])

            @pl.when(y == 0)
            def _():
                def one(i, carry):
                    skip_back(i)
                    return carry

                lax.fori_loop(0, 4, one, 0)

            landed(din, hop_r.at[1])
            cur[...] = din[...].astype(F32)

            def step_back(n, carry):
                i = 3 - n

                @pl.when(y == 1)
                def _():
                    skip_back(i)

                d_full = cur[...] + pre[i]
                d_low = back(i, d_full.astype(BF16), d_full)
                send_part(R, i, RB, rp_s, rp_r)
                cur[...] = d_low.astype(F32)
                return carry

            lax.fori_loop(0, 4, step_back, 0)

            @pl.when(y == 1)
            def _():
                xout[...] = cur[...].astype(BF16)
                remote(xout, din, hop_s.at[1], hop_r.at[1], down).start()

    @pl.when(jnp.logical_not(encoder))
    def _():
        wait_weights(0)
        wait_weights(1)
        wait_weights(2)

        @pl.when(worker)
        def _():
            cond = condition()

            def skip_in(i):
                landed(L.at[i, 2], sk_r.at[i])
                pre[i] = dot(L[i, 2], W[2, i])

            @pl.when(y == 3)
            def _():
                def one(i, carry):
                    skip_in(i)
                    return carry

                lax.fori_loop(0, 4, one, 0)

            landed(xin, hop_r.at[0])
            cur[...] = xin[...].astype(F32)

            def step(i, carry):
                @pl.when(y == 2)
                def _():
                    skip_in(i)

                cur[...] = activate(i, cur[...] + pre[i], cond).astype(F32)
                return carry

            lax.fori_loop(0, 4, step, 0)

            @pl.when(y == 2)
            def _():
                xout[...] = cur[...].astype(BF16)
                remote(xout, xin, hop_s.at[0], hop_r.at[0], up).start()

            give_left()

        @pl.when(y == 2)
        def _():
            order_left()

        @pl.when(worker)
        def _():
            @pl.when(y == 3)
            def _():
                cur[...] = dbuf[...].astype(F32)

            @pl.when(y == 2)
            def _():
                landed(din, hop_r.at[1])
                cur[...] = din[...].astype(F32)

            def step_back(n, carry):
                i = 3 - n
                d_full = cur[...]
                g = back(i, d_full.astype(BF16), d_full)
                R[i, 2] = g
                cur[...] = g.astype(F32)
                send_part(R, i, RB, rp_s, rp_r)
                return carry

            lax.fori_loop(0, 4, step_back, 0)
            remote(R.at[0, 2], din, hop_s.at[1], hop_r.at[1], down).start()

            def give_q(i, carry):
                skout[i] = dot_rhs_t(R[i, 2], W[2, i]).astype(BF16)
                remote(
                    skout.at[i], R.at[3 - i, 2], q_s.at[i], q_r.at[3 - i], across
                ).start()
                return carry

            lax.fori_loop(0, 4, give_q, 0)

        @pl.when(y == 3)
        def _():
            order_left()

    for m in range(MB):
        landed(RB.at[m], rp_r.at[m])
    grads = [dot_lhs_t(LP[kind], stacked(RB, kind)) for kind in range(3)]
    for c in range(NZ):
        for h in range(2):
            g_in, g_out, g_skip = (g[48 * c + 24 * h : 48 * c + 24 * h + 24] for g in grads)
            pm[c, 64 * h : 64 * h + 16] = g_in[:16]
            pm[c, 64 * h + 16 : 64 * h + 24] = g_in[16:] + g_out[:8]
            pm[c, 64 * h + 24 : 64 * h + 40] = g_out[8:]
            pm[c, 64 * h + 40 : 64 * h + 64] = g_skip

    half = NZ // 2
    other = 1 - xh

    def at(side, step):
        return (side, (z + step + NZ) % NZ, y, xl, co)

    def rows_of(h):
        return pl.ds(pl.multiple_of(64 * h, 64), 64)

    cross[...] = pm[z, rows_of(other)].astype(BF16)
    remote(cross, fin.at[4], fin_s.at[4], fin_r.at[4], at(other, 0)).start()

    def hop(way, t, first):
        sbuf, rbuf, ssem, rsem = ((sbp, rbp, sps, rps), (sbm, rbm, sms, rms))[way]
        chunk = ((z + half - t) if way == 0 else (z - half + 1 + t + NZ)) % NZ
        for k in range(4):
            rows = pl.ds(32 * k, 32)
            total = pm[chunk, 32 * k : 32 * k + 32]
            if not first:
                landed(rbuf.at[t - 1, rows], rsem.at[t - 1, k])
                total = total + rbuf[t - 1, 32 * k : 32 * k + 32].astype(F32)
            sbuf[t, 32 * k : 32 * k + 32] = total.astype(BF16)
            remote(
                sbuf.at[t, rows],
                rbuf.at[t, rows],
                ssem.at[t, k],
                rsem.at[t, k],
                at(xh, 1 - 2 * way),
            ).start()

    def last_hop(way, t):
        rbuf, rsem, buf = ((rbp, rps, lastp), (rbm, rms, lastm))[way]
        for k in range(4):
            landed(rbuf.at[t - 1, pl.ds(32 * k, 32)], rsem.at[t - 1, k])
        chunk = (z + 1 - 2 * way + NZ) % NZ
        buf[...] = (pm[chunk] + rbuf[t - 1].astype(F32)).astype(BF16)
        for n, side in enumerate((other, xh)):
            slot = 2 * way + n
            remote(
                buf.at[rows_of(side)],
                fin.at[slot],
                fin_s.at[slot],
                fin_r.at[slot],
                at(side, 1 - 2 * way),
            ).start()

    hop(0, 0, True)
    hop(1, 0, True)

    def ring_step(t, carry):
        hop(0, t, False)
        hop(1, t, False)
        return carry

    lax.fori_loop(1, half - 2, ring_step, 0)
    hop(0, half - 2, False)
    last_hop(1, half - 2)
    last_hop(0, half - 1)
    own = pm[z, rows_of(xh)]
    for slot in (4, 3, 2):
        landed(fin.at[slot], fin_r.at[slot])
        own = own + fin[slot].astype(F32)
    out_a[...] = own[:60].reshape(60, 1, C)
    for slot in (1, 0):
        landed(fin.at[slot], fin_r.at[slot])
    rest = fin[0].astype(F32) + fin[1].astype(F32)
    out_b[...] = rest[:60].reshape(60, 1, C)

    chain_sent()
    landed(cross, fin_s.at[4])
    for slot in range(4):
        landed(cross, fin_s.at[slot])

    def left_ring(t, carry):
        for k in range(4):
            landed(sbp.at[0, pl.ds(0, 32)], sps.at[t, k])
        return carry

    lax.fori_loop(0, half - 1, left_ring, 0)

    def left_ring_back(t, carry):
        for k in range(4):
            landed(sbm.at[0, pl.ds(0, 32)], sms.at[t, k])
        return carry

    lax.fori_loop(0, half - 2, left_ring_back, 0)


def on_device(features, timesteps, text_ids, text_table, w_in, w_out, w_skip, cotangent):
    dma = pltpu.SemaphoreType.DMA
    half = NZ // 2

    def bf(*shape):
        return pltpu.VMEM(shape, BF16)

    def f32(*shape):
        return pltpu.VMEM(shape, F32)

    block = (ROWS, C)
    scratch = [
        pltpu.VMEM(text_ids.shape[::-1], jnp.int32),
        bf(*text_table.shape),
        bf(3, 4, C, C),
        f32(*block),
        bf(*block),
        bf(*block),
        bf(*block),
        bf(*block),
        bf(*block),
        bf(4, *block),
        f32(4, *block),
        bf(4, 3, *block),
        bf(4, 3, *block),
        f32(4, *block),
        f32(4, 8, C),
        bf(MB, 3, *block),
        bf(MB, 3, *block),
        bf(3, MB * ROWS, 2 * NZ * 24),
        bf(C, C),
        bf(C, 2 * NZ * 24),
        bf(C, 2 * NZ * 24),
        f32(2 * MB, 16, C),
        bf(2 * MB, 16, C),
        bf(8, 16, C),
        bf(16, C),
        bf(4, 16, C),
        f32(NZ, 1, C),
        f32(NZ, 1, C),
        f32(NZ, 128, C),
        bf(half - 1, 128, C),
        bf(half - 1, 128, C),
        bf(half - 2, 128, C),
        bf(half - 2, 128, C),
        bf(128, C),
        bf(128, C),
        bf(64, C),
        bf(5, 64, C),
        dma((4,)),
        dma((3,)),
        dma((3,)),
        dma((3,)),
        dma((3, 2)),
        dma((3, 2)),
        dma((3, 2)),
        dma((3, 2)),
        dma((2 * MB,)),
        dma((8,)),
        dma((4,)),
        dma((4,)),
        dma((NZ,)),
        dma((NZ,)),
        dma((2,)),
        dma((2,)),
        dma((4,)),
        dma((4,)),
        dma((4,)),
        dma((4,)),
        dma((4,)),
        dma((MB,)),
        dma((4,)),
        dma((MB,)),
        dma((half - 1, 4)),
        dma((half - 1, 4)),
        dma((half - 2, 4)),
        dma((half - 2, 4)),
        dma((5,)),
        dma((5,)),
    ]
    vmem = pl.BlockSpec(memory_space=pltpu.VMEM)
    hbm = pl.BlockSpec(memory_space=pl.ANY)
    sums = jax.ShapeDtypeStruct((60, 1, C), F32)
    first, second = pl.pallas_call(
        kernel,
        out_shape=(sums, sums),
        in_specs=[pl.BlockSpec(memory_space=pltpu.SMEM)] + [hbm] * 7,
        out_specs=(vmem, vmem),
        scratch_shapes=scratch,
        compiler_params=pltpu.CompilerParams(
            collective_id=0, has_side_effects=True, vmem_limit_bytes=56 * 2**20
        ),
        name="unet_step",
    )(timesteps, features, text_ids.T, text_table, w_in, w_out, w_skip, cotangent)
    return tuple(
        jnp.transpose(first[20 * k : 20 * k + 20] + second[20 * k : 20 * k + 20], (1, 0, 2))
        for k in range(3)
    )


def solution(mesh):
    split_mesh = Mesh(mesh.devices.reshape(2, NZ, 4, 2, 2), AXES)
    weight = P(SEG, None, None)
    return jax.shard_map(
        on_device,
        mesh=split_mesh,
        in_specs=(
            P(DP, None),
            P(DP),
            P(),
            P(DP + SEG, None),
            weight,
            weight,
            weight,
            P(DP, None),
        ),
        out_specs=(P(SEG, DP, None),) * 3,
        check_vma=False,
    )
```

```python
import math

import jax
import jax.numpy as jnp
from jax import lax
from jax.experimental import pallas as pl
from jax.experimental.pallas import tpu as pltpu
from jax.sharding import Mesh
from jax.sharding import PartitionSpec as P

C = 640
ROWS = 64
GROUPS = 32
MB = 3
NZ = 16
BF16 = jnp.bfloat16
F32 = jnp.float32
AXES = ("xh", "z", "y", "xl", "co")
DP = ("xh", "z")
SEG = ("y", "xl", "co")
MESH = pl.DeviceIdType.MESH
EPSILON = 1e-05


def dot(a, b):
    return jnp.dot(a, b, preferred_element_type=F32)


def dot_lhs_t(a, b):
    return lax.dot_general(a, b, (((0,), (0,)), ((), ())), preferred_element_type=F32)


def iota(shape, dim):
    return lax.broadcasted_iota(jnp.int32, shape, dim)


def split(v, terms):
    out = []
    for _ in range(terms):
        part = v.astype(BF16)
        out.append(part)
        v = v - part.astype(F32)
    return out


def group_means(sums, terms, group_matrix):
    parts = [p for s in sums for p in split(s, terms)]
    pad = jnp.zeros((16 - len(parts), C), BF16)
    prod = dot(jnp.concatenate(parts + [pad], axis=0), group_matrix)
    out = []
    for k in range(len(sums)):
        total = prod[k * terms : k * terms + 1]
        for t in range(1, terms):
            total = total + prod[k * terms + t : k * terms + t + 1]
        out.append(total * (1.0 / (ROWS * (C // GROUPS))))
    return out


def normalize(v, about, group_matrix):
    v = v - about
    mean, square = group_means(
        [jnp.sum(v, axis=0, keepdims=True), jnp.sum(v * v, axis=0, keepdims=True)],
        3,
        group_matrix,
    )
    inv = lax.rsqrt(jnp.maximum(square - mean * mean, 0.0) + EPSILON)
    return (v - mean) * inv, inv, about + mean


def normalize_back(v, normed, inv, group_matrix):
    m1, m2 = group_means(
        [jnp.sum(v, axis=0, keepdims=True), jnp.sum(v * normed, axis=0, keepdims=True)],
        2,
        group_matrix,
    )
    return inv * (v - m1 - normed * m2)


def landed(ref, sem):
    pltpu.make_async_copy(ref, ref, sem).wait()


def kernel(
    steps,
    feat,
    ids_in,
    table_in,
    w_in,
    w_out,
    w_skip,
    cot,
    out_a,
    out_b,
    ids,
    table,
    W,
    WT,
    shift,
    cur,
    xbuf,
    dbuf,
    xin,
    din,
    xout,
    skout,
    pre,
    L,
    R,
    sp,
    inv_std,
    LB,
    RB,
    LP,
    gmat,
    s_low,
    s_high,
    p0f,
    p0b,
    c1,
    c2s,
    c2,
    c3s,
    c3,
    pm,
    sbp,
    rbp,
    sbm,
    rbm,
    lastp,
    lastm,
    cross,
    fin,
    in_sem,
    wl,
    wcs,
    wcr,
    wxs,
    wxr,
    wfs,
    wfr,
    c1s_sem,
    c1r_sem,
    c2s_sem,
    c2r_sem,
    c3s_sem,
    c3r_sem,
    hop_s,
    hop_r,
    sk_s,
    sk_r,
    q_s,
    q_r,
    lp_s,
    lp_r,
    rp_s,
    rp_r,
    sps,
    rps,
    sms,
    rms,
    fin_s,
    fin_r,
    reach,
):
    xh, z, y = lax.axis_index("xh"), lax.axis_index("z"), lax.axis_index("y")
    xl, co = lax.axis_index("xl"), lax.axis_index("co")
    j = xl * 2 + co
    p = xh * 4 + j
    weights = (w_in, w_out, w_skip)
    sample = jnp.minimum(j, MB - 1)
    worker = j < MB
    def remote(src, dst, ssem, rsem, dev):
        return pltpu.make_async_remote_copy(
            src_ref=src,
            dst_ref=dst,
            send_sem=ssem,
            recv_sem=rsem,
            device_id=dev,
            device_id_type=MESH,
        )

    for kind in range(3):
        pltpu.make_async_copy(weights[kind].at[0], W.at[kind, j], wl.at[kind]).start()
    pltpu.make_async_copy(ids_in, ids, in_sem.at[2]).start()
    pltpu.make_async_copy(table_in, table, in_sem.at[3]).start()
    rows = pl.ds(pl.multiple_of(sample * ROWS, ROWS), ROWS)
    pltpu.make_async_copy(feat.at[rows], xbuf, in_sem.at[0]).start()
    pltpu.make_async_copy(cot.at[rows], dbuf, in_sem.at[1]).start()

    barrier = pltpu.get_barrier_semaphore()

    def greet(dev):
        pl.semaphore_signal(barrier, inc=1, device_id=dev, device_id_type=MESH)

    for d in range(1, 8):
        q = (p + d) % 8
        greet((q // 4, z, y, (q // 2) % 2, q % 2))
    for d in range(1, 4):
        greet((xh, z, (y + d) % 4, xl, co))
    for side in (1, NZ - 1):
        greet((1 - xh, (z + side) % NZ, y, xl, co))

    for d in (1, 2, 3, 4):
        greet((xh, (z + d) % NZ, y, xl, co))
        greet((xh, (z + NZ - d) % NZ, y, xl, co))

    landed(ids, in_sem.at[2])
    landed(table, in_sem.at[3])
    base = ((((xh * NZ + z) * 4 + y) * 4) + j) * table.shape[0]
    tokens = ids[...] - base
    words = table.shape[0]
    row = iota((words, 96), 0)

    def count(n, acc):
        for u in range(8):
            v = n * 8 + u
            hits = jnp.sum(jnp.where(tokens == v, 1.0, 0.0), axis=0, keepdims=True)
            acc = jnp.where(row == v, hits, acc)
        return acc

    counts = lax.fori_loop(0, words // 8, count, jnp.zeros((words, 96), F32))
    r96 = iota((1, 96), 1)
    place = (r96 // 48) * 48 + (r96 % 16) * MB + (r96 % 48) // 16
    order = jnp.where(place == iota((96, 1), 0), 1.0, 0.0).astype(BF16)
    counts = dot(counts.astype(BF16), order).astype(BF16)
    part = dot_lhs_t(counts, table[...]) * (1.0 / ids.shape[0])
    p0f[...] = part.reshape(2 * MB, 16, C)
    p0b[...] = p0f[...].astype(BF16)

    pl.semaphore_wait(barrier, 7 + 3 + 2 + 8)
    for d in (4, NZ - 4):
        pl.semaphore_signal(
            reach, inc=1, device_id=(xh, (z + d) % NZ, y, xl, co), device_id_type=MESH
        )

    core_dev = (xh, z, y, xl, 1 - co)
    x_devs = ((xh, z, y, 1 - xl, co), (1 - xh, z, y, 1 - xl, co))
    quarter = C // 4
    quarters = [[pl.ds((2 * h + n) * quarter, quarter) for n in range(2)] for h in range(2)]
    far = 2 * (1 - xl) + co

    def start_weights(kind, n):
        for h in range(2):
            rows = quarters[h][n]
            remote(
                weights[kind].at[0, rows],
                W.at[kind, j, rows],
                wxs.at[kind, h, n],
                wxr.at[kind, h, n],
                x_devs[h],
            ).start()
        if n == 1:
            remote(
                weights[kind].at[0], W.at[kind, j], wcs.at[kind], wcr.at[kind], core_dev
            ).start()

    def relay_weights(kind):
        for n in range(2):
            for h in range(2):
                block = W.at[kind, far, quarters[h][n]]
                landed(block, wxr.at[kind, h, n])
                remote(
                    block, block, wfs.at[kind, h, n], wfr.at[kind, h, n], core_dev
                ).start()

    def wait_weights(kind):
        landed(W.at[kind, 0], wl.at[kind])
        landed(W.at[kind, 0], wcr.at[kind])
        for h in range(2):
            for n in range(2):
                landed(W.at[kind, 0, quarters[h][n]], wfr.at[kind, h, n])

    def startup_sent():
        for b in range(2 * MB):
            bx, bj = b // MB, b % MB

            @pl.when(p != 4 * bx + bj)
            def _():
                landed(p0b.at[0], c1s_sem.at[b])

        @pl.when(worker)
        def _():
            for d in range(1, 4):
                landed(c2s, c2s_sem.at[d])

            def given(d, carry):
                q = (z + d) % NZ
                landed(c3s.at[q], c3s_sem.at[q])
                return carry

            lax.fori_loop(1, NZ, given, 0)

        for kind in range(3):
            landed(W.at[kind, 0], wcs.at[kind])
            for h in range(2):
                for n in range(2):
                    landed(W.at[kind, 0, quarters[h][n]], wxs.at[kind, h, n])
                    landed(W.at[kind, 0, quarters[h][n]], wfs.at[kind, h, n])

    def condition():
        lane = iota((1, C), 1)
        half_width = C // 2
        k = jnp.where(lane < half_width, lane, lane - half_width).astype(F32)
        freqs = jnp.exp(-math.log(10000.0) * k / half_width)
        angles = steps[sample].astype(F32) * freqs
        total = jnp.where(lane < half_width, jnp.cos(angles), jnp.sin(angles)) + c3s[z]

        def add(d, acc):
            q = (z + d) % NZ
            landed(c3.at[q], c3r_sem.at[q])
            return acc + c3[q]

        return lax.fori_loop(1, NZ, add, total)

    for b in range(2 * MB):
        bx, bj = b // MB, b % MB

        @pl.when(p != 4 * bx + bj)
        def _():
            remote(
                p0b.at[b],
                c1.at[p],
                c1s_sem.at[b],
                c1r_sem.at[p],
                (bx, z, y, bj // 2, bj % 2),
            ).start()

    start_weights(0, 0)
    gmat[...] = jnp.where(
        iota((C, 1), 0) // (C // GROUPS) == iota((1, C), 1) // (C // GROUPS), 1.0, 0.0
    ).astype(BF16)

    @pl.when(worker)
    def _():
        acc = p0f[xh * MB + sample]
        for d in range(1, 8):
            q = (p + d) % 8
            landed(c1.at[q], c1r_sem.at[q])
            acc = acc + c1[q].astype(F32)
        c2s[...] = acc.astype(BF16)
        for d in range(1, 4):
            remote(
                c2s, c2.at[y], c2s_sem.at[d], c2r_sem.at[y], (xh, z, (y + d) % 4, xl, co)
            ).start()
        start_weights(0, 1)
        for d in range(1, 4):
            q = (y + d) % 4
            landed(c2.at[q], c2r_sem.at[q])
            acc = acc + c2[q].astype(F32)
        pl.semaphore_wait(reach, 2)
        for r in range(NZ):
            c3s[r] = acc[r : r + 1]

        def give(d, carry):
            q = (z + d) % NZ
            remote(
                c3s.at[q], c3.at[z], c3s_sem.at[q], c3r_sem.at[z], (xh, q, y, xl, co)
            ).start()
            return carry

        lax.fori_loop(1, NZ, give, 0)

    @pl.when(jnp.logical_not(worker))
    def _():
        start_weights(0, 1)
        pl.semaphore_wait(reach, 2)

    start_weights(1, 0)
    start_weights(1, 1)
    relay_weights(0)
    relay_weights(1)
    start_weights(2, 0)
    start_weights(2, 1)

    @pl.when(y >= 2)
    def _():
        relay_weights(2)

    landed(xbuf, in_sem.at[0])
    landed(dbuf, in_sem.at[1])


    def chain_sent():
        startup_sent()

        @pl.when(worker)
        def _():
            done_part(L, lp_s)
            done_part(R, rp_s)

            def sent(i, carry):
                @pl.when(encoder)
                def _():
                    landed(skout.at[i], sk_s.at[i])

                @pl.when(jnp.logical_not(encoder))
                def _():
                    landed(skout.at[i], q_s.at[i])

                return carry

            lax.fori_loop(0, 4, sent, 0)

            @pl.when(y < 3)
            def _():
                landed(xout, hop_s.at[0])

            @pl.when(y > 0)
            def _():
                landed(xout, hop_s.at[1])

    def activate(i, v, cond):
        normed, inv, shift[...] = normalize(v, shift[...], gmat[...])
        low = normed.astype(BF16)
        L[i, 0] = low
        inv_std[i] = jnp.broadcast_to(inv, (8, C))
        act = dot(low, W[0, i]) + cond
        sig = 1.0 / (1.0 + jnp.exp(-act))
        hidden = (act * sig).astype(BF16)
        L[i, 1] = hidden
        sp[i] = sig * (1.0 + act * (1.0 - sig))
        return (v + dot(hidden, W[1, i])).astype(BF16)

    def start_shift(v):
        (shift[...],) = group_means([jnp.sum(v, axis=0, keepdims=True)], 3, gmat[...])

    def back(i, d_low, d_full):
        R[i, 1] = d_low
        e = (dot(d_low, WT[1, i]) * sp[i]).astype(BF16)
        R[i, 0] = e
        v = dot(e, WT[0, i])
        g = normalize_back(v, L[i, 0].astype(F32), inv_std[i, 0:1], gmat[...])
        return (d_full + g).astype(BF16)

    def send_part(buf, i, dst, ssem, rsem):
        @pl.when(i == j)
        def _():
            pltpu.make_async_copy(buf.at[i], dst.at[sample], rsem.at[sample]).start()

        @pl.when(i != j)
        def _():
            remote(
                buf.at[i],
                dst.at[sample],
                ssem.at[i],
                rsem.at[sample],
                (xh, z, y, i // 2, i % 2),
            ).start()

    def done_part(buf, ssem):
        def one(i, carry):
            @pl.when(i != j)
            def _():
                landed(buf.at[i], ssem.at[i])

            return carry

        lax.fori_loop(0, 4, one, 0)

    up = (xh, z, (y + 1) % 4, xl, co)
    down = (xh, z, (y + 3) % 4, xl, co)
    across = (xh, z, 3 - y, xl, co)
    encoder = y < 2

    def transpose_weights():
        def one(i, carry):
            for kind in range(3):
                WT[kind, i] = W[kind, i].T
            return carry

        lax.fori_loop(0, 4, one, 0)

    def give_left():
        def one(i, carry):
            send_part(L, i, LB, lp_s, lp_r)
            return carry

        lax.fori_loop(0, 4, one, 0)

    def stacked(ref, kind):
        return jnp.concatenate([ref[m, kind] for m in range(MB)], axis=0)

    def order_left():
        col = iota((1, 2 * NZ * 24), 1)
        block, off = col // 24, col % 24
        first = (block % 2) * (C // 2) + (block // 2) * 20
        row = iota((C, 1), 0)
        low = jnp.where(off < 20, first + off, -1)
        high = jnp.where(off >= 4, first + off - 4, -1)
        s_low[...] = jnp.where(row == low, 1.0, 0.0).astype(BF16)
        s_high[...] = jnp.where(row == high, 1.0, 0.0).astype(BF16)
        for m in range(MB):
            landed(LB.at[m], lp_r.at[m])
        for kind, order in enumerate((s_low, s_high, s_low)):
            LP[kind] = dot(stacked(LB, kind), order[...]).astype(BF16).T

    @pl.when(encoder)
    def _():
        @pl.when(worker)
        def _():
            cond = condition()
            wait_weights(0)
            wait_weights(1)

            @pl.when(y == 0)
            def _():
                cur[...] = xbuf[...].astype(F32)

            @pl.when(y == 1)
            def _():
                landed(xin, hop_r.at[0])
                cur[...] = xin[...].astype(F32)

            start_shift(cur[...])

            def step(i, carry):
                result = activate(i, cur[...], cond)
                L[i, 2] = result
                cur[...] = result.astype(F32)
                return carry

            lax.fori_loop(0, 4, step, 0)
            remote(L.at[3, 2], xin, hop_s.at[0], hop_r.at[0], up).start()

        @pl.when(jnp.logical_not(worker))
        def _():
            wait_weights(0)
            wait_weights(1)

        relay_weights(2)
        wait_weights(2)

        @pl.when(worker)
        def _():
            def give_skip(n, carry):
                i = 3 - n
                skout[i] = dot(L[i, 2], W[2, i]).astype(BF16)
                remote(
                    skout.at[i], L.at[3 - i, 2], sk_s.at[i], sk_r.at[3 - i], across
                ).start()
                return carry

            lax.fori_loop(0, 4, give_skip, 0)
            give_left()

        order_left()

        @pl.when(worker)
        def _():
            transpose_weights()

            def skip_back(i):
                landed(R.at[i, 2], q_r.at[i])
                pre[i] = dot(R[i, 2], WT[2, i])

            @pl.when(y == 0)
            def _():
                def one(i, carry):
                    skip_back(i)
                    return carry

                lax.fori_loop(0, 4, one, 0)

            landed(din, hop_r.at[1])
            cur[...] = din[...].astype(F32)

            def step_back(n, carry):
                i = 3 - n

                @pl.when(y == 1)
                def _():
                    skip_back(i)

                d_full = cur[...] + pre[i]
                d_low = back(i, d_full.astype(BF16), d_full)
                send_part(R, i, RB, rp_s, rp_r)
                cur[...] = d_low.astype(F32)
                return carry

            lax.fori_loop(0, 4, step_back, 0)

            @pl.when(y == 1)
            def _():
                xout[...] = cur[...].astype(BF16)
                remote(xout, din, hop_s.at[1], hop_r.at[1], down).start()

    @pl.when(jnp.logical_not(encoder))
    def _():
        wait_weights(0)
        wait_weights(1)
        wait_weights(2)

        @pl.when(worker)
        def _():
            cond = condition()
            transpose_weights()

            def skip_in(i):
                landed(L.at[i, 2], sk_r.at[i])
                pre[i] = dot(L[i, 2], W[2, i])

            @pl.when(y == 3)
            def _():
                def one(i, carry):
                    skip_in(i)
                    return carry

                lax.fori_loop(0, 4, one, 0)

            landed(xin, hop_r.at[0])
            cur[...] = xin[...].astype(F32)

            @pl.when(y == 2)
            def _():
                skip_in(0)

            start_shift(cur[...] + pre[0])

            def step(i, carry):
                @pl.when(jnp.logical_and(y == 2, i > 0))
                def _():
                    skip_in(i)

                cur[...] = activate(i, cur[...] + pre[i], cond).astype(F32)
                return carry

            lax.fori_loop(0, 4, step, 0)

            @pl.when(y == 2)
            def _():
                xout[...] = cur[...].astype(BF16)
                remote(xout, xin, hop_s.at[0], hop_r.at[0], up).start()

            give_left()

        @pl.when(y == 2)
        def _():
            order_left()

        @pl.when(worker)
        def _():
            @pl.when(y == 3)
            def _():
                cur[...] = dbuf[...].astype(F32)

            @pl.when(y == 2)
            def _():
                landed(din, hop_r.at[1])
                cur[...] = din[...].astype(F32)

            def step_back(n, carry):
                i = 3 - n
                d_full = cur[...]
                g = back(i, d_full.astype(BF16), d_full)
                R[i, 2] = g
                cur[...] = g.astype(F32)
                send_part(R, i, RB, rp_s, rp_r)
                return carry

            lax.fori_loop(0, 4, step_back, 0)
            remote(R.at[0, 2], din, hop_s.at[1], hop_r.at[1], down).start()

            def give_q(i, carry):
                skout[i] = dot(R[i, 2], WT[2, i]).astype(BF16)
                remote(
                    skout.at[i], R.at[3 - i, 2], q_s.at[i], q_r.at[3 - i], across
                ).start()
                return carry

            lax.fori_loop(0, 4, give_q, 0)

        @pl.when(y == 3)
        def _():
            order_left()

    for m in range(MB):
        landed(RB.at[m], rp_r.at[m])
    grads = [dot(LP[kind], stacked(RB, kind)) for kind in range(3)]
    for c in range(NZ):
        for h in range(2):
            g_in, g_out, g_skip = (g[48 * c + 24 * h : 48 * c + 24 * h + 24] for g in grads)
            pm[c, 64 * h : 64 * h + 16] = g_in[:16]
            pm[c, 64 * h + 16 : 64 * h + 24] = g_in[16:] + g_out[:8]
            pm[c, 64 * h + 24 : 64 * h + 40] = g_out[8:]
            pm[c, 64 * h + 40 : 64 * h + 64] = g_skip

    half = NZ // 2
    other = 1 - xh

    def at(side, step):
        return (side, (z + step + NZ) % NZ, y, xl, co)

    def rows_of(h):
        return pl.ds(pl.multiple_of(64 * h, 64), 64)

    cross[...] = pm[z, rows_of(other)].astype(BF16)
    remote(cross, fin.at[4], fin_s.at[4], fin_r.at[4], at(other, 0)).start()

    def hop(ways, t, first):
        for k in range(4):
            rows = pl.ds(32 * k, 32)
            for way in ways:
                sbuf, rbuf, ssem, rsem = ((sbp, rbp, sps, rps), (sbm, rbm, sms, rms))[way]
                chunk = ((z + half - t) if way == 0 else (z - half + 1 + t + NZ)) % NZ
                total = pm[chunk, 32 * k : 32 * k + 32]
                if not first:
                    landed(rbuf.at[t - 1, rows], rsem.at[t - 1, k])
                    total = total + rbuf[t - 1, 32 * k : 32 * k + 32].astype(F32)
                sbuf[t, 32 * k : 32 * k + 32] = total.astype(BF16)
                remote(
                    sbuf.at[t, rows],
                    rbuf.at[t, rows],
                    ssem.at[t, k],
                    rsem.at[t, k],
                    at(xh, 1 - 2 * way),
                ).start()

    def last_hop(way, t):
        rbuf, rsem, buf = ((rbp, rps, lastp), (rbm, rms, lastm))[way]
        for k in range(4):
            landed(rbuf.at[t - 1, pl.ds(32 * k, 32)], rsem.at[t - 1, k])
        chunk = (z + 1 - 2 * way + NZ) % NZ
        buf[...] = (pm[chunk] + rbuf[t - 1].astype(F32)).astype(BF16)
        for n, side in enumerate((other, xh)):
            slot = 2 * way + n
            remote(
                buf.at[rows_of(side)],
                fin.at[slot],
                fin_s.at[slot],
                fin_r.at[slot],
                at(side, 1 - 2 * way),
            ).start()

    hop((0, 1), 0, True)

    def ring_step(t, carry):
        hop((0, 1), t, False)
        return carry

    lax.fori_loop(1, half - 2, ring_step, 0)
    hop((0,), half - 2, False)
    last_hop(1, half - 2)
    last_hop(0, half - 1)
    own = pm[z, rows_of(xh)]
    for slot in (4, 3, 2):
        landed(fin.at[slot], fin_r.at[slot])
        own = own + fin[slot].astype(F32)
    out_a[...] = own[:60].reshape(60, 1, C)
    for slot in (1, 0):
        landed(fin.at[slot], fin_r.at[slot])
    rest = fin[0].astype(F32) + fin[1].astype(F32)
    out_b[...] = rest[:60].reshape(60, 1, C)

    chain_sent()
    landed(cross, fin_s.at[4])
    for slot in range(4):
        landed(cross, fin_s.at[slot])

    def left_ring(t, carry):
        for k in range(4):
            landed(sbp.at[0, pl.ds(0, 32)], sps.at[t, k])
        return carry

    lax.fori_loop(0, half - 1, left_ring, 0)

    def left_ring_back(t, carry):
        for k in range(4):
            landed(sbm.at[0, pl.ds(0, 32)], sms.at[t, k])
        return carry

    lax.fori_loop(0, half - 2, left_ring_back, 0)


def on_device(features, timesteps, text_ids, text_table, w_in, w_out, w_skip, cotangent):
    dma = pltpu.SemaphoreType.DMA
    half = NZ // 2

    def bf(*shape):
        return pltpu.VMEM(shape, BF16)

    def f32(*shape):
        return pltpu.VMEM(shape, F32)

    block = (ROWS, C)
    scratch = [
        pltpu.VMEM(text_ids.shape[::-1], jnp.int32),
        bf(*text_table.shape),
        bf(3, 4, C, C),
        bf(3, 4, C, C),
        f32(1, C),
        f32(*block),
        bf(*block),
        bf(*block),
        bf(*block),
        bf(*block),
        bf(*block),
        bf(4, *block),
        f32(4, *block),
        bf(4, 3, *block),
        bf(4, 3, *block),
        f32(4, *block),
        f32(4, 8, C),
        bf(MB, 3, *block),
        bf(MB, 3, *block),
        bf(3, 2 * NZ * 24, MB * ROWS),
        bf(C, C),
        bf(C, 2 * NZ * 24),
        bf(C, 2 * NZ * 24),
        f32(2 * MB, 16, C),
        bf(2 * MB, 16, C),
        bf(8, 16, C),
        bf(16, C),
        bf(4, 16, C),
        f32(NZ, 1, C),
        f32(NZ, 1, C),
        f32(NZ, 128, C),
        bf(half - 1, 128, C),
        bf(half - 1, 128, C),
        bf(half - 2, 128, C),
        bf(half - 2, 128, C),
        bf(128, C),
        bf(128, C),
        bf(64, C),
        bf(5, 64, C),
        dma((4,)),
        dma((3,)),
        dma((3,)),
        dma((3,)),
        dma((3, 2, 2)),
        dma((3, 2, 2)),
        dma((3, 2, 2)),
        dma((3, 2, 2)),
        dma((2 * MB,)),
        dma((8,)),
        dma((4,)),
        dma((4,)),
        dma((NZ,)),
        dma((NZ,)),
        dma((2,)),
        dma((2,)),
        dma((4,)),
        dma((4,)),
        dma((4,)),
        dma((4,)),
        dma((4,)),
        dma((MB,)),
        dma((4,)),
        dma((MB,)),
        dma((half - 1, 4)),
        dma((half - 1, 4)),
        dma((half - 2, 4)),
        dma((half - 2, 4)),
        dma((5,)),
        dma((5,)),
        pltpu.SemaphoreType.REGULAR,
    ]
    vmem = pl.BlockSpec(memory_space=pltpu.VMEM)
    hbm = pl.BlockSpec(memory_space=pl.ANY)
    sums = jax.ShapeDtypeStruct((60, 1, C), F32)
    first, second = pl.pallas_call(
        kernel,
        out_shape=(sums, sums),
        in_specs=[pl.BlockSpec(memory_space=pltpu.SMEM)] + [hbm] * 7,
        out_specs=(vmem, vmem),
        scratch_shapes=scratch,
        compiler_params=pltpu.CompilerParams(
            collective_id=0, has_side_effects=True, vmem_limit_bytes=56 * 2**20
        ),
        name="unet_step",
    )(timesteps, features, text_ids.T, text_table, w_in, w_out, w_skip, cotangent)
    return tuple(
        jnp.transpose(first[20 * k : 20 * k + 20] + second[20 * k : 20 * k + 20], (1, 0, 2))
        for k in range(3)
    )


def solution(mesh):
    split_mesh = Mesh(mesh.devices.reshape(2, NZ, 4, 2, 2), AXES)
    weight = P(SEG, None, None)
    return jax.shard_map(
        on_device,
        mesh=split_mesh,
        in_specs=(
            P(DP, None),
            P(DP),
            P(),
            P(DP + SEG, None),
            weight,
            weight,
            weight,
            P(DP, None),
        ),
        out_specs=(P(SEG, DP, None),) * 3,
        check_vma=False,
    )
```

```python
import math

import jax
import jax.numpy as jnp
from jax import lax
from jax.experimental import pallas as pl
from jax.experimental.pallas import tpu as pltpu
from jax.sharding import Mesh
from jax.sharding import PartitionSpec as P

C = 640
ROWS = 64
GROUPS = 32
MB = 3
NZ = 16
BF16 = jnp.bfloat16
F32 = jnp.float32
AXES = ("xh", "z", "y", "xl", "co")
DP = ("xh", "z")
SEG = ("y", "xl", "co")
MESH = pl.DeviceIdType.MESH
EPSILON = 1e-05


def dot(a, b):
    return jnp.dot(a, b, preferred_element_type=F32)


def dot_lhs_t(a, b):
    return lax.dot_general(a, b, (((0,), (0,)), ((), ())), preferred_element_type=F32)


def iota(shape, dim):
    return lax.broadcasted_iota(jnp.int32, shape, dim)


def split(v, terms):
    out = []
    for _ in range(terms):
        part = v.astype(BF16)
        out.append(part)
        v = v - part.astype(F32)
    return out


def group_means(sums, terms, group_matrix):
    parts = [p for s in sums for p in split(s, terms)]
    pad = jnp.zeros((16 - len(parts), C), BF16)
    prod = dot(jnp.concatenate(parts + [pad], axis=0), group_matrix)
    out = []
    for k in range(len(sums)):
        total = prod[k * terms : k * terms + 1]
        for t in range(1, terms):
            total = total + prod[k * terms + t : k * terms + t + 1]
        out.append(total * (1.0 / (ROWS * (C // GROUPS))))
    return out


def normalize(v, about, group_matrix):
    v = v - about
    mean, square = group_means(
        [jnp.sum(v, axis=0, keepdims=True), jnp.sum(v * v, axis=0, keepdims=True)],
        3,
        group_matrix,
    )
    inv = lax.rsqrt(jnp.maximum(square - mean * mean, 0.0) + EPSILON)
    return (v - mean) * inv, inv, about + mean


def normalize_back(v, normed, inv, group_matrix):
    m1, m2 = group_means(
        [jnp.sum(v, axis=0, keepdims=True), jnp.sum(v * normed, axis=0, keepdims=True)],
        2,
        group_matrix,
    )
    return inv * (v - m1 - normed * m2)


def landed(ref, sem):
    pltpu.make_async_copy(ref, ref, sem).wait()


def kernel(
    steps,
    feat,
    ids_in,
    table_in,
    w_in,
    w_out,
    w_skip,
    cot,
    out_a,
    out_b,
    ids,
    table,
    W,
    WT,
    shift,
    cur,
    xbuf,
    dbuf,
    xin,
    din,
    xout,
    skout,
    pre,
    L,
    R,
    R2,
    sp,
    inv_std,
    LB,
    RB,
    RB2,
    LP,
    gmat,
    s_low,
    s_high,
    p0f,
    p0b,
    c1,
    c2s,
    c2,
    c3s,
    c3,
    pm,
    sbp,
    rbp,
    sbm,
    rbm,
    lastp,
    lastm,
    cross,
    fin,
    in_sem,
    wl,
    wcs,
    wcr,
    wxs,
    wxr,
    wfs,
    wfr,
    c1s_sem,
    c1r_sem,
    c2s_sem,
    c2r_sem,
    c3s_sem,
    c3r_sem,
    hop_s,
    hop_r,
    sk_s,
    sk_r,
    q_s,
    q_r,
    lp_s,
    lp_r,
    rp_s,
    rp_r,
    kp_s,
    kp_r,
    sps,
    rps,
    sms,
    rms,
    fin_s,
    fin_r,
    reach,
):
    xh, z, y = lax.axis_index("xh"), lax.axis_index("z"), lax.axis_index("y")
    xl, co = lax.axis_index("xl"), lax.axis_index("co")
    j = xl * 2 + co
    p = xh * 4 + j
    weights = (w_in, w_out, w_skip)
    sample = jnp.minimum(j, MB - 1)
    worker = j < MB
    def remote(src, dst, ssem, rsem, dev):
        return pltpu.make_async_remote_copy(
            src_ref=src,
            dst_ref=dst,
            send_sem=ssem,
            recv_sem=rsem,
            device_id=dev,
            device_id_type=MESH,
        )

    for kind in range(3):
        pltpu.make_async_copy(weights[kind].at[0], W.at[kind, j], wl.at[kind]).start()
    pltpu.make_async_copy(ids_in, ids, in_sem.at[2]).start()
    pltpu.make_async_copy(table_in, table, in_sem.at[3]).start()
    rows = pl.ds(pl.multiple_of(sample * ROWS, ROWS), ROWS)
    pltpu.make_async_copy(feat.at[rows], xbuf, in_sem.at[0]).start()
    pltpu.make_async_copy(cot.at[rows], dbuf, in_sem.at[1]).start()

    barrier = pltpu.get_barrier_semaphore()

    def greet(dev):
        pl.semaphore_signal(barrier, inc=1, device_id=dev, device_id_type=MESH)

    for d in range(1, 8):
        q = (p + d) % 8
        greet((q // 4, z, y, (q // 2) % 2, q % 2))
    for d in range(1, 4):
        greet((xh, z, (y + d) % 4, xl, co))
    for side in (1, NZ - 1):
        greet((1 - xh, (z + side) % NZ, y, xl, co))

    for d in (1, 2, 3, 4):
        greet((xh, (z + d) % NZ, y, xl, co))
        greet((xh, (z + NZ - d) % NZ, y, xl, co))

    landed(ids, in_sem.at[2])
    landed(table, in_sem.at[3])
    base = ((((xh * NZ + z) * 4 + y) * 4) + j) * table.shape[0]
    tokens = ids[...] - base
    words = table.shape[0]
    row = iota((words, 96), 0)

    def count(n, acc):
        for u in range(8):
            v = n * 8 + u
            hits = jnp.sum(jnp.where(tokens == v, 1.0, 0.0), axis=0, keepdims=True)
            acc = jnp.where(row == v, hits, acc)
        return acc

    counts = lax.fori_loop(0, words // 8, count, jnp.zeros((words, 96), F32))
    r96 = iota((1, 96), 1)
    place = (r96 // 48) * 48 + (r96 % 16) * MB + (r96 % 48) // 16
    order = jnp.where(place == iota((96, 1), 0), 1.0, 0.0).astype(BF16)
    counts = dot(counts.astype(BF16), order).astype(BF16)
    part = dot_lhs_t(counts, table[...]) * (1.0 / ids.shape[0])
    p0f[...] = part.reshape(2 * MB, 16, C)
    p0b[...] = p0f[...].astype(BF16)

    pl.semaphore_wait(barrier, 7 + 3 + 2 + 8)
    for d in (4, NZ - 4):
        pl.semaphore_signal(
            reach, inc=1, device_id=(xh, (z + d) % NZ, y, xl, co), device_id_type=MESH
        )

    core_dev = (xh, z, y, xl, 1 - co)
    x_devs = ((xh, z, y, 1 - xl, co), (1 - xh, z, y, 1 - xl, co))
    quarter = C // 4
    quarters = [[pl.ds((2 * h + n) * quarter, quarter) for n in range(2)] for h in range(2)]
    far = 2 * (1 - xl) + co

    def start_weights(kind, n):
        for h in range(2):
            rows = quarters[h][n]
            remote(
                weights[kind].at[0, rows],
                W.at[kind, j, rows],
                wxs.at[kind, h, n],
                wxr.at[kind, h, n],
                x_devs[h],
            ).start()
        if n == 1:
            remote(
                weights[kind].at[0], W.at[kind, j], wcs.at[kind], wcr.at[kind], core_dev
            ).start()

    def relay_weights(kind):
        for n in range(2):
            for h in range(2):
                block = W.at[kind, far, quarters[h][n]]
                landed(block, wxr.at[kind, h, n])
                remote(
                    block, block, wfs.at[kind, h, n], wfr.at[kind, h, n], core_dev
                ).start()

    def wait_weights(kind):
        landed(W.at[kind, 0], wl.at[kind])
        landed(W.at[kind, 0], wcr.at[kind])
        for h in range(2):
            for n in range(2):
                landed(W.at[kind, 0, quarters[h][n]], wfr.at[kind, h, n])

    def startup_sent():
        for b in range(2 * MB):
            bx, bj = b // MB, b % MB

            @pl.when(p != 4 * bx + bj)
            def _():
                landed(p0b.at[0], c1s_sem.at[b])

        @pl.when(worker)
        def _():
            for d in range(1, 4):
                landed(c2s, c2s_sem.at[d])

            def given(d, carry):
                q = (z + d) % NZ
                landed(c3s.at[q], c3s_sem.at[q])
                return carry

            lax.fori_loop(1, NZ, given, 0)

        for kind in range(3):
            landed(W.at[kind, 0], wcs.at[kind])
            for h in range(2):
                for n in range(2):
                    landed(W.at[kind, 0, quarters[h][n]], wxs.at[kind, h, n])
                    landed(W.at[kind, 0, quarters[h][n]], wfs.at[kind, h, n])

    def condition():
        lane = iota((1, C), 1)
        half_width = C // 2
        k = jnp.where(lane < half_width, lane, lane - half_width).astype(F32)
        freqs = jnp.exp(-math.log(10000.0) * k / half_width)
        angles = steps[sample].astype(F32) * freqs
        total = jnp.where(lane < half_width, jnp.cos(angles), jnp.sin(angles)) + c3s[z]

        def add(d, acc):
            q = (z + d) % NZ
            landed(c3.at[q], c3r_sem.at[q])
            return acc + c3[q]

        return lax.fori_loop(1, NZ, add, total)

    for b in range(2 * MB):
        bx, bj = b // MB, b % MB

        @pl.when(p != 4 * bx + bj)
        def _():
            remote(
                p0b.at[b],
                c1.at[p],
                c1s_sem.at[b],
                c1r_sem.at[p],
                (bx, z, y, bj // 2, bj % 2),
            ).start()

    start_weights(0, 0)
    gmat[...] = jnp.where(
        iota((C, 1), 0) // (C // GROUPS) == iota((1, C), 1) // (C // GROUPS), 1.0, 0.0
    ).astype(BF16)

    @pl.when(worker)
    def _():
        acc = p0f[xh * MB + sample]
        for d in range(1, 8):
            q = (p + d) % 8
            landed(c1.at[q], c1r_sem.at[q])
            acc = acc + c1[q].astype(F32)
        c2s[...] = acc.astype(BF16)
        for d in range(1, 4):
            remote(
                c2s, c2.at[y], c2s_sem.at[d], c2r_sem.at[y], (xh, z, (y + d) % 4, xl, co)
            ).start()
        start_weights(0, 1)
        for d in range(1, 4):
            q = (y + d) % 4
            landed(c2.at[q], c2r_sem.at[q])
            acc = acc + c2[q].astype(F32)
        pl.semaphore_wait(reach, 2)
        for r in range(NZ):
            c3s[r] = acc[r : r + 1]

        def give(d, carry):
            q = (z + d) % NZ
            remote(
                c3s.at[q], c3.at[z], c3s_sem.at[q], c3r_sem.at[z], (xh, q, y, xl, co)
            ).start()
            return carry

        lax.fori_loop(1, NZ, give, 0)

    @pl.when(jnp.logical_not(worker))
    def _():
        start_weights(0, 1)
        pl.semaphore_wait(reach, 2)

    start_weights(1, 0)
    start_weights(1, 1)

    def start_skip_weights():
        start_weights(2, 0)
        start_weights(2, 1)

    relay_weights(0)
    relay_weights(1)
    start_skip_weights()

    @pl.when(y >= 2)
    def _():
        relay_weights(2)

    landed(xbuf, in_sem.at[0])
    landed(dbuf, in_sem.at[1])


    def chain_sent():
        startup_sent()

        @pl.when(worker)
        def _():
            done_part(L.at[0], lp_s)
            done_part(R.at[0], rp_s)
            done_part(R2.at[0], kp_s)

            def sent(i, carry):
                @pl.when(encoder)
                def _():
                    landed(skout.at[i], sk_s.at[i])

                @pl.when(jnp.logical_not(encoder))
                def _():
                    landed(skout.at[i], q_s.at[i])

                return carry

            lax.fori_loop(0, 4, sent, 0)

            @pl.when(y < 3)
            def _():
                landed(xout, hop_s.at[0])

            @pl.when(y > 0)
            def _():
                landed(xout, hop_s.at[1])

    def activate(i, v, cond):
        normed, inv, shift[...] = normalize(v, shift[...], gmat[...])
        low = normed.astype(BF16)
        L[i, 0] = low
        inv_std[i] = jnp.broadcast_to(inv, (8, C))
        act = dot(low, W[0, i]) + cond
        sig = 1.0 / (1.0 + jnp.exp(-act))
        hidden = (act * sig).astype(BF16)
        L[i, 1] = hidden
        sp[i] = sig * (1.0 + act * (1.0 - sig))
        return (v + dot(hidden, W[1, i])).astype(BF16)

    def start_shift(v):
        (shift[...],) = group_means([jnp.sum(v, axis=0, keepdims=True)], 3, gmat[...])

    def back(i, d_low, d_full):
        R[i, 1] = d_low
        e = (dot(d_low, WT[1, i]) * sp[i]).astype(BF16)
        R[i, 0] = e
        v = dot(e, WT[0, i])
        g = normalize_back(v, L[i, 0].astype(F32), inv_std[i, 0:1], gmat[...])
        return (d_full + g).astype(BF16)

    def send_part(src, dst, i, ssem, rsem):
        @pl.when(i == j)
        def _():
            pltpu.make_async_copy(src, dst, rsem).start()

        @pl.when(i != j)
        def _():
            remote(src, dst, ssem, rsem, (xh, z, y, i // 2, i % 2)).start()

    def send_right(i):
        send_part(R.at[i], RB.at[sample], i, rp_s.at[i], rp_r.at[sample])

    def send_right_skip(i):
        send_part(R2.at[i], RB2.at[sample], i, kp_s.at[i], kp_r.at[sample])

    def done_part(like, ssem):
        def one(i, carry):
            @pl.when(i != j)
            def _():
                landed(like, ssem.at[i])

            return carry

        lax.fori_loop(0, 4, one, 0)

    up = (xh, z, (y + 1) % 4, xl, co)
    down = (xh, z, (y + 3) % 4, xl, co)
    across = (xh, z, 3 - y, xl, co)
    encoder = y < 2

    def transpose_weights():
        def one(i, carry):
            for kind in range(3):
                WT[kind, i] = W[kind, i].T
            return carry

        lax.fori_loop(0, 4, one, 0)

    def give_left():
        def one(i, carry):
            send_part(L.at[i], LB.at[sample], i, lp_s.at[i], lp_r.at[sample])
            return carry

        lax.fori_loop(0, 4, one, 0)

    def stacked(ref, kind):
        return jnp.concatenate([ref[m, kind] for m in range(MB)], axis=0)

    def order_left():
        col = iota((1, 2 * NZ * 24), 1)
        block, off = col // 24, col % 24
        first = (block % 2) * (C // 2) + (block // 2) * 20
        row = iota((C, 1), 0)
        low = jnp.where(off < 20, first + off, -1)
        high = jnp.where(off >= 4, first + off - 4, -1)
        s_low[...] = jnp.where(row == low, 1.0, 0.0).astype(BF16)
        s_high[...] = jnp.where(row == high, 1.0, 0.0).astype(BF16)
        for m in range(MB):
            landed(LB.at[m], lp_r.at[m])
        for kind, order in enumerate((s_low, s_high, s_low)):
            LP[kind] = dot(stacked(LB, kind), order[...]).astype(BF16).T

    def each(first, count, fn):
        def one(i, carry):
            fn(i)
            return carry

        lax.fori_loop(first, count, one, 0)

    def give_skip(i):
        skout[i] = dot(L[i, 2], W[2, i]).astype(BF16)
        remote(skout.at[i], L.at[3 - i, 2], sk_s.at[i], sk_r.at[3 - i], across).start()

    def give_q(i):
        skout[i] = dot(R2[i], WT[2, i]).astype(BF16)
        remote(skout.at[i], R2.at[3 - i], q_s.at[i], q_r.at[3 - i], across).start()

    @pl.when(encoder)
    def _():
        @pl.when(worker)
        def _():
            cond = condition()
            wait_weights(0)
            wait_weights(1)

            @pl.when(y == 0)
            def _():
                cur[...] = xbuf[...].astype(F32)

            @pl.when(y == 1)
            def _():
                landed(xin, hop_r.at[0])
                cur[...] = xin[...].astype(F32)

            start_shift(cur[...])

            def step(i, carry):
                result = activate(i, cur[...], cond)
                L[i, 2] = result
                cur[...] = result.astype(F32)

                return carry

            lax.fori_loop(0, 4, step, 0)
            remote(L.at[3, 2], xin, hop_s.at[0], hop_r.at[0], up).start()

        @pl.when(jnp.logical_not(worker))
        def _():
            wait_weights(0)
            wait_weights(1)

        relay_weights(2)
        wait_weights(2)

        @pl.when(worker)
        def _():
            each(0, 4, lambda n: give_skip(3 - n))
            give_left()

        order_left()

        @pl.when(worker)
        def _():
            transpose_weights()

            def skip_back(i):
                landed(R2.at[i], q_r.at[i])
                pre[i] = dot(R2[i], WT[2, i])

            @pl.when(y == 0)
            def _():
                def ahead(i):
                    skip_back(i)
                    send_right_skip(i)

                each(0, 4, ahead)

            landed(din, hop_r.at[1])
            cur[...] = din[...].astype(F32)

            def step_back(n, carry):
                i = 3 - n

                @pl.when(y == 1)
                def _():
                    skip_back(i)
                    send_right_skip(i)

                d_full = cur[...] + pre[i]
                d_low = back(i, d_full.astype(BF16), d_full)

                send_right(i)
                cur[...] = d_low.astype(F32)
                return carry

            lax.fori_loop(0, 4, step_back, 0)

            @pl.when(y == 1)
            def _():
                xout[...] = cur[...].astype(BF16)
                remote(xout, din, hop_s.at[1], hop_r.at[1], down).start()

    @pl.when(jnp.logical_not(encoder))
    def _():
        wait_weights(0)
        wait_weights(1)
        wait_weights(2)

        @pl.when(worker)
        def _():
            cond = condition()
            transpose_weights()

            def skip_in(i):
                landed(L.at[i, 2], sk_r.at[i])
                pre[i] = dot(L[i, 2], W[2, i])

            @pl.when(y == 3)
            def _():
                each(0, 4, skip_in)

            landed(xin, hop_r.at[0])
            cur[...] = xin[...].astype(F32)

            @pl.when(y == 2)
            def _():
                skip_in(0)

            start_shift(cur[...] + pre[0])

            def step(i, carry):
                @pl.when(jnp.logical_and(y == 2, i > 0))
                def _():
                    skip_in(i)

                cur[...] = activate(i, cur[...] + pre[i], cond).astype(F32)
                return carry

            lax.fori_loop(0, 4, step, 0)

            @pl.when(y == 2)
            def _():
                xout[...] = cur[...].astype(BF16)
                remote(xout, xin, hop_s.at[0], hop_r.at[0], up).start()

            give_left()

        @pl.when(y == 2)
        def _():
            order_left()

        @pl.when(worker)
        def _():
            @pl.when(y == 3)
            def _():
                cur[...] = dbuf[...].astype(F32)

            @pl.when(y == 2)
            def _():
                landed(din, hop_r.at[1])
                cur[...] = din[...].astype(F32)

            def step_back(n, carry):
                i = 3 - n
                d_full = cur[...]
                g = back(i, d_full.astype(BF16), d_full)
                R2[i] = g
                cur[...] = g.astype(F32)
                send_right_skip(i)
                send_right(i)

                return carry

            lax.fori_loop(0, 4, step_back, 0)
            remote(R2.at[0], din, hop_s.at[1], hop_r.at[1], down).start()
            each(0, 4, give_q)

        @pl.when(y == 3)
        def _():
            order_left()

    for m in range(MB):
        landed(RB2.at[m], kp_r.at[m])
        landed(RB.at[m], rp_r.at[m])
    grads = [dot(LP[kind], stacked(RB, kind)) for kind in range(2)]
    grads.append(dot(LP[2], jnp.concatenate([RB2[m] for m in range(MB)], axis=0)))
    for c in range(NZ):
        for h in range(2):
            g_in, g_out, g_skip = (g[48 * c + 24 * h : 48 * c + 24 * h + 24] for g in grads)
            pm[c, 64 * h : 64 * h + 16] = g_in[:16]
            pm[c, 64 * h + 16 : 64 * h + 24] = g_in[16:] + g_out[:8]
            pm[c, 64 * h + 24 : 64 * h + 40] = g_out[8:]
            pm[c, 64 * h + 40 : 64 * h + 64] = g_skip

    half = NZ // 2
    other = 1 - xh

    def at(side, step):
        return (side, (z + step + NZ) % NZ, y, xl, co)

    def rows_of(h):
        return pl.ds(pl.multiple_of(64 * h, 64), 64)

    cross[...] = pm[z, rows_of(other)].astype(BF16)
    remote(cross, fin.at[4], fin_s.at[4], fin_r.at[4], at(other, 0)).start()

    def hop(ways, t, first):
        for k in range(4):
            rows = pl.ds(32 * k, 32)
            for way in ways:
                sbuf, rbuf, ssem, rsem = ((sbp, rbp, sps, rps), (sbm, rbm, sms, rms))[way]
                chunk = ((z + half - t) if way == 0 else (z - half + 1 + t + NZ)) % NZ
                total = pm[chunk, 32 * k : 32 * k + 32]
                if not first:
                    landed(rbuf.at[t - 1, rows], rsem.at[t - 1, k])
                    total = total + rbuf[t - 1, 32 * k : 32 * k + 32].astype(F32)
                sbuf[t, 32 * k : 32 * k + 32] = total.astype(BF16)
                remote(
                    sbuf.at[t, rows],
                    rbuf.at[t, rows],
                    ssem.at[t, k],
                    rsem.at[t, k],
                    at(xh, 1 - 2 * way),
                ).start()

    def last_hop(way, t):
        rbuf, rsem, buf = ((rbp, rps, lastp), (rbm, rms, lastm))[way]
        for k in range(4):
            landed(rbuf.at[t - 1, pl.ds(32 * k, 32)], rsem.at[t - 1, k])
        chunk = (z + 1 - 2 * way + NZ) % NZ
        buf[...] = (pm[chunk] + rbuf[t - 1].astype(F32)).astype(BF16)
        for n, side in enumerate((other, xh)):
            slot = 2 * way + n
            remote(
                buf.at[rows_of(side)],
                fin.at[slot],
                fin_s.at[slot],
                fin_r.at[slot],
                at(side, 1 - 2 * way),
            ).start()

    hop((0, 1), 0, True)

    def ring_step(t, carry):
        hop((0, 1), t, False)
        return carry

    lax.fori_loop(1, half - 2, ring_step, 0)
    hop((0,), half - 2, False)
    last_hop(1, half - 2)
    last_hop(0, half - 1)
    own = pm[z, rows_of(xh)]
    for slot in (4, 3, 2):
        landed(fin.at[slot], fin_r.at[slot])
        own = own + fin[slot].astype(F32)
    out_a[...] = own[:60].reshape(60, 1, C)
    for slot in (1, 0):
        landed(fin.at[slot], fin_r.at[slot])
    rest = fin[0].astype(F32) + fin[1].astype(F32)
    out_b[...] = rest[:60].reshape(60, 1, C)

    chain_sent()
    landed(cross, fin_s.at[4])
    for slot in range(4):
        landed(cross, fin_s.at[slot])

    def left_ring(t, carry):
        for k in range(4):
            landed(sbp.at[0, pl.ds(0, 32)], sps.at[t, k])
        return carry

    lax.fori_loop(0, half - 1, left_ring, 0)

    def left_ring_back(t, carry):
        for k in range(4):
            landed(sbm.at[0, pl.ds(0, 32)], sms.at[t, k])
        return carry

    lax.fori_loop(0, half - 2, left_ring_back, 0)


def on_device(features, timesteps, text_ids, text_table, w_in, w_out, w_skip, cotangent):
    dma = pltpu.SemaphoreType.DMA
    half = NZ // 2

    def bf(*shape):
        return pltpu.VMEM(shape, BF16)

    def f32(*shape):
        return pltpu.VMEM(shape, F32)

    block = (ROWS, C)
    scratch = [
        pltpu.VMEM(text_ids.shape[::-1], jnp.int32),
        bf(*text_table.shape),
        bf(3, 4, C, C),
        bf(3, 4, C, C),
        f32(1, C),
        f32(*block),
        bf(*block),
        bf(*block),
        bf(*block),
        bf(*block),
        bf(*block),
        bf(4, *block),
        f32(4, *block),
        bf(4, 3, *block),
        bf(4, 2, *block),
        bf(4, *block),
        f32(4, *block),
        f32(4, 8, C),
        bf(MB, 3, *block),
        bf(MB, 2, *block),
        bf(MB, *block),
        bf(3, 2 * NZ * 24, MB * ROWS),
        bf(C, C),
        bf(C, 2 * NZ * 24),
        bf(C, 2 * NZ * 24),
        f32(2 * MB, 16, C),
        bf(2 * MB, 16, C),
        bf(8, 16, C),
        bf(16, C),
        bf(4, 16, C),
        f32(NZ, 1, C),
        f32(NZ, 1, C),
        f32(NZ, 128, C),
        bf(half - 1, 128, C),
        bf(half - 1, 128, C),
        bf(half - 2, 128, C),
        bf(half - 2, 128, C),
        bf(128, C),
        bf(128, C),
        bf(64, C),
        bf(5, 64, C),
        dma((4,)),
        dma((3,)),
        dma((3,)),
        dma((3,)),
        dma((3, 2, 2)),
        dma((3, 2, 2)),
        dma((3, 2, 2)),
        dma((3, 2, 2)),
        dma((2 * MB,)),
        dma((8,)),
        dma((4,)),
        dma((4,)),
        dma((NZ,)),
        dma((NZ,)),
        dma((2,)),
        dma((2,)),
        dma((4,)),
        dma((4,)),
        dma((4,)),
        dma((4,)),
        dma((4,)),
        dma((MB,)),
        dma((4,)),
        dma((MB,)),
        dma((4,)),
        dma((MB,)),
        dma((half - 1, 4)),
        dma((half - 1, 4)),
        dma((half - 2, 4)),
        dma((half - 2, 4)),
        dma((5,)),
        dma((5,)),
        pltpu.SemaphoreType.REGULAR,
    ]
    vmem = pl.BlockSpec(memory_space=pltpu.VMEM)
    hbm = pl.BlockSpec(memory_space=pl.ANY)
    sums = jax.ShapeDtypeStruct((60, 1, C), F32)
    first, second = pl.pallas_call(
        kernel,
        out_shape=(sums, sums),
        in_specs=[pl.BlockSpec(memory_space=pltpu.SMEM)] + [hbm] * 7,
        out_specs=(vmem, vmem),
        scratch_shapes=scratch,
        compiler_params=pltpu.CompilerParams(
            collective_id=0, has_side_effects=True, vmem_limit_bytes=56 * 2**20
        ),
        name="unet_step",
    )(timesteps, features, text_ids.T, text_table, w_in, w_out, w_skip, cotangent)
    return tuple(
        jnp.transpose(first[20 * k : 20 * k + 20] + second[20 * k : 20 * k + 20], (1, 0, 2))
        for k in range(3)
    )


def solution(mesh):
    split_mesh = Mesh(mesh.devices.reshape(2, NZ, 4, 2, 2), AXES)
    weight = P(SEG, None, None)
    return jax.shard_map(
        on_device,
        mesh=split_mesh,
        in_specs=(
            P(DP, None),
            P(DP),
            P(),
            P(DP + SEG, None),
            weight,
            weight,
            weight,
            P(DP, None),
        ),
        out_specs=(P(SEG, DP, None),) * 3,
        check_vma=False,
    )
```
